32 devices in a mesh: shot: 4 (over x, core), dom: 8 (over z, y).
Axes of the slice: x: 2, y: 2, z: 4, core: 2. Of those that a mesh axis runs over, the one named last changes fastest.
Arguments:
- parked: bfloat16 [4, 64, 32768], P('shot', 'dom'), may hold values from -6 to 6
- parked_slot: int32 [4, 8, 8], P('shot', 'dom'), may hold values from 0 to 7, as said below
- holder_list: int32 [4, 8, 8], P('shot', 'dom'), may hold values from 0 to 7, as said below
- speed_sq: float32 [64, 128, 128], P('dom'), may hold values from 0.04 to 0.18
- adjoint_next: float32 [4, 64, 128, 128], P('shot', 'dom'), may hold values from -6 to 6
- adjoint_now: float32 [4, 64, 128, 128], P('shot', 'dom'), may hold values from -6 to 6
- wavelet: float32 [4, 3], P('shot'), may hold values from -9 to 9
- src_depth: int32 [4], P('shot'), may hold values from 0 to 63
- src_row: int32 [4], P('shot'), may hold values from 0 to 16383
- rec_depth: int32 [1024], replicated, may hold values from 0 to 63
- rec_row: int32 [1024], replicated, may hold values from 0 to 16383
- residuals: float32 [4, 4, 1024], P('shot'), may hold values from -6 to 6
Outputs:
- gradient: float32 [64, 128, 128], P('dom', 'shot')
- adjoint_late: float32 [4, 64, 128, 128], P('shot', 'dom')
- adjoint_early: float32 [4, 64, 128, 128], P('shot', 'dom')
The draws below stay inside these ranges and needn't reach their ends.
Inputs may be any that keep to these rules, and one draw needn't show every extreme that they name: Each row of parked_slot names every slot of its holder once. Each row of holder_list names every holder slab once.
All inputs are finite; a program needn't handle non-finite values.
Results may differ from the reference program's by a relative error of at most 0.0005.
Values may be sent and summed in bfloat16 or wider, within the bound.
A program may use at most 64 MiB of HBM per device.

```python
import math
import jax
import jax.numpy as jnp
import numpy as np
from jax import lax

DZ = 8
NX = 128
NY = 128
NREC = 1024
STEPS = 4
SHOTS = 4
NZ = 64
PIECE = 32768
N_DOM = 8


two_pi = 2.0 * math.pi


def shuffle_row(row_key):
    return jax.random.permutation(row_key, N_DOM).astype(jnp.int32)


def owner_layout(key):
    slot_keys = jax.random.split(jax.random.fold_in(key, 101), SHOTS * N_DOM)
    holder_keys = jax.random.split(jax.random.fold_in(key, 102), SHOTS * N_DOM)
    slot_table = jax.vmap(shuffle_row)(slot_keys).reshape(SHOTS, N_DOM, N_DOM)
    holder_table = jax.vmap(shuffle_row)(holder_keys).reshape(SHOTS, N_DOM, N_DOM)
    return (slot_table, holder_table)


def draw_parked_slot(key, part):
    return owner_layout(key)[0]


def draw_holder_list(key, part):
    return owner_layout(key)[1]


def per_shot(values, rank_of):
    return values.reshape((SHOTS,) + (1,) * (rank_of - 1))


def wave_factor(position, period, offset_by):
    phase_idx = jnp.remainder(position + offset_by, period).astype(jnp.float32)
    return jnp.cos(phase_idx * (two_pi / period.astype(jnp.float32)))


def smooth_part(wave_key, depth_at, lateral_x, lateral_y, level_lo, level_hi):
    rank_of = depth_at.ndim
    periods = jax.random.randint(jax.random.fold_in(wave_key, 1), (3, 3, SHOTS), 8, 17).astype(jnp.int32)
    offsets = jax.random.randint(jax.random.fold_in(wave_key, 2), (3, 3, SHOTS), 0, 64).astype(jnp.int32)
    amplitudes = jax.random.uniform(jax.random.fold_in(wave_key, 3), (3, SHOTS), jnp.float32, -0.6, 0.6)
    mean_level = jax.random.uniform(jax.random.fold_in(wave_key, 4), (SHOTS,), jnp.float32, level_lo, level_hi)
    summed = per_shot(mean_level, rank_of)
    for wave_num in range(3):
        factor = per_shot(amplitudes[wave_num], rank_of)
        factor = factor * wave_factor(depth_at, per_shot(periods[wave_num, 0], rank_of), per_shot(offsets[wave_num, 0], rank_of))
        factor = factor * wave_factor(lateral_x, per_shot(periods[wave_num, 1], rank_of), per_shot(offsets[wave_num, 1], rank_of))
        factor = factor * wave_factor(lateral_y, per_shot(periods[wave_num, 2], rank_of), per_shot(offsets[wave_num, 2], rank_of))
        summed = summed + factor
    return summed


def rough_part(rough_key, shape_of, flat_law):
    if flat_law:
        return jax.random.uniform(rough_key, shape_of, jnp.float32, -0.85, 0.85)
    else:
        return 0.5 * jax.random.truncated_normal(rough_key, -3.0, 3.0, shape_of, jnp.float32)


def adjoint_field(key, rough_num, level_lo, level_hi, flat_law):
    depth_at = jnp.arange(NZ, dtype=jnp.int32).reshape(1, NZ, 1, 1)
    lateral_x = jnp.arange(NX, dtype=jnp.int32).reshape(1, 1, NX, 1)
    lateral_y = jnp.arange(NY, dtype=jnp.int32).reshape(1, 1, 1, NY)
    smooth = smooth_part(jax.random.fold_in(key, 41), depth_at, lateral_x, lateral_y, level_lo, level_hi)
    rough = rough_part(jax.random.fold_in(key, rough_num), (SHOTS, NZ, NX, NY), flat_law)
    return (smooth + rough).astype(jnp.float32)


def draw_adjoint_next(key, part):
    return adjoint_field(key, 51, 1.0, 2.0, False)


def draw_adjoint_now(key, part):
    return adjoint_field(key, 52, 1.0, 2.0, False)


def take_rows(field_rows, source_row):
    return jnp.take(field_rows, source_row, axis=0)


def parked_field(key, level_lo, level_hi, flat_law):
    planes = jnp.arange(N_DOM, dtype=jnp.int32)[:, None] * DZ + jnp.arange(DZ, dtype=jnp.int32)[None, :]
    depth_at = planes.reshape(1, N_DOM, 1, DZ, 1, 1)
    lateral_x = jnp.arange(NX, dtype=jnp.int32).reshape(1, 1, 1, 1, NX, 1)
    lateral_y = jnp.arange(NY, dtype=jnp.int32).reshape(1, 1, 1, 1, 1, NY)
    smooth = smooth_part(jax.random.fold_in(key, 42), depth_at, lateral_x, lateral_y, level_lo, level_hi)
    field = smooth + rough_part(jax.random.fold_in(key, 53), (SHOTS, N_DOM, 2, DZ, NX, NY), flat_law)
    field_rows = field.reshape(SHOTS, N_DOM * N_DOM, PIECE)
    slot_table, holder_table = owner_layout(key)
    owner_of_row = jnp.argsort(slot_table, axis=-1).astype(jnp.int32).reshape(SHOTS, N_DOM * N_DOM)
    piece_table = jnp.argsort(holder_table, axis=-1).astype(jnp.int32).reshape(SHOTS, N_DOM * N_DOM)
    holder_of_row = (jnp.arange(N_DOM * N_DOM, dtype=jnp.int32) // N_DOM)[None, :]
    piece_of_row = jnp.take_along_axis(piece_table, owner_of_row * N_DOM + holder_of_row, axis=1)
    source_row = (owner_of_row * N_DOM + piece_of_row).astype(jnp.int32)
    parked_rows = jax.vmap(take_rows)(field_rows, source_row)
    return parked_rows.astype(jnp.bfloat16)


def draw_parked(key, part):
    return parked_field(key, 1.0, 2.0, False)


def place_ends(array, stream_key, low, top_value):
    dims = array.shape
    spot = [jax.random.randint(jax.random.fold_in(stream_key, axis), (), 0, dims[axis]) for axis in range(len(dims))]
    array = array.at[tuple(spot)].set(low)
    longest = dims.index(max(dims))
    spot[longest] = (spot[longest] + 1) % dims[longest]
    return array.at[tuple(spot)].set(top_value)


def steps_of(own_key, dims, cuts, least, high):
    def one(dim, blocks):
        heights = jax.random.uniform(jax.random.fold_in(jax.random.fold_in(own_key, 6), dim), (blocks,), jnp.float32, least / len(cuts), high / len(cuts))
        return jnp.repeat(jnp.exp(heights), dims[dim] // blocks).reshape((-1,) + (1,) * (len(dims) - dim - 1))

    loudness = one(*cuts[0])
    for cut in cuts[1:]:
        loudness = loudness * one(*cut)
    return loudness


def rank_table(count, lean):
    portions = [(1 << 20) // math.isqrt(grade ** lean) + 1 for grade in range(1, count + 1)]
    spread = 1 + sum(portions) // (1 << 30)
    return np.cumsum(np.array([max(1, weight // spread) for weight in portions]))


def ranked_ids(stream_key, extent, count, skew):
    table = rank_table(count, skew)
    pick = jax.random.randint(jax.random.fold_in(stream_key, 1), extent, 0, int(table[count - 1]))
    rank = jnp.searchsorted(jnp.asarray(table, jnp.int32), pick, side="right")
    return jax.random.permutation(jax.random.fold_in(stream_key, 2), count)[rank].astype(jnp.int32)


def scatter_about(rng, shape, spread, reach, shards=(), held_as=jnp.bfloat16):
    loudness = steps_of(rng, shape, shards, -0.22, 0.18) if shards else 1.0
    values = jax.random.normal(rng, shape, jnp.float32) * spread * loudness
    return jnp.minimum(jnp.maximum(values, -reach), reach).astype(held_as)


def setup_inputs(seed: int = 0) -> dict:
    key_list = jax.random.split(jax.random.key(seed), 13)
    return {
        "parked": draw_parked(jax.random.fold_in(key_list[12], 71), 0),
        "parked_slot": draw_parked_slot(jax.random.fold_in(key_list[12], 71), 0),
        "holder_list": draw_holder_list(jax.random.fold_in(key_list[12], 71), 0),
        "speed_sq": jnp.clip(jnp.exp(math.log(0.18) - 1.50407746 * jax.random.uniform(key_list[3], (NZ, NX, NY), jnp.float32) ** steps_of(key_list[3], (NZ, NX, NY), ((0, 8),), -0.2, 0.2)), 0.04, 0.18),
        "adjoint_next": draw_adjoint_next(jax.random.fold_in(key_list[12], 71), 0),
        "adjoint_now": draw_adjoint_now(jax.random.fold_in(key_list[12], 71), 0),
        "wavelet": scatter_about(key_list[6], (SHOTS, STEPS - 1), 3.0, 9.0, ((0, 4),), jnp.float32),
        "src_depth": place_ends(jax.random.randint(key_list[7], (SHOTS,), 0, NZ), jax.random.fold_in(key_list[7], 1), 0, NZ - 1).astype(jnp.int32),
        "src_row": place_ends(jax.random.randint(key_list[8], (SHOTS,), 0, NX * NY), jax.random.fold_in(key_list[8], 1), 0, (NX * NY) - 1).astype(jnp.int32),
        "rec_depth": place_ends(ranked_ids(key_list[9], (NREC,), NZ, 2), jax.random.fold_in(key_list[9], 3), 0, NZ - 1).astype(jnp.int32),
        "rec_row": place_ends(jax.random.randint(key_list[10], (NREC,), 0, NX * NY), jax.random.fold_in(key_list[10], 1), 0, (NX * NY) - 1).astype(jnp.int32),
        "residuals": scatter_about(key_list[11], (SHOTS, STEPS, NREC), 1.0, 6.0, ((0, 4),), jnp.float32),
    }


stencil_coef = (-205.0 / 72.0, 8.0 / 5.0, -1.0 / 5.0, 8.0 / 315.0, -1.0 / 560.0)
grad_scale = 0.0625


def shifted(field, offset, axis_num):
    widths = [(0, 0), (0, 0), (0, 0)]
    widths[axis_num] = (4, 4)
    padded = jnp.pad(field, widths)
    return lax.slice_in_dim(padded, 4 + offset, 4 + offset + field.shape[axis_num], axis=axis_num)


def laplace(field):
    summed = 3.0 * stencil_coef[0] * field
    for offset in range(1, 5):
        neighbours = shifted(field, offset, 0) + shifted(field, -offset, 0)
        neighbours = neighbours + shifted(field, offset, 1) + shifted(field, -offset, 1)
        neighbours = neighbours + shifted(field, offset, 2) + shifted(field, -offset, 2)
        summed = summed + stencil_coef[offset] * neighbours
    return summed


def inject(field, depth_at, row_at, amount):
    flat_index = depth_at * (NX * NY) + row_at
    updated = field.reshape(-1).at[flat_index].add(amount)
    return updated.reshape(field.shape)


def reference(parked, parked_slot, holder_list, speed_sq, adjoint_next, adjoint_now, wavelet, src_depth, src_row, rec_depth, rec_row, residuals):
    owners = jnp.arange(N_DOM, dtype=jnp.int32)
    gradient = jnp.zeros((NZ, NX, NY), jnp.float32)
    late_list = []
    early_list = []
    for shot_index in range(SHOTS):
        holders = holder_list[shot_index]
        slot_ids = parked_slot[shot_index][holders, owners[:, None]]
        row_ids = (holders * N_DOM + slot_ids).astype(jnp.int32)
        pieces = parked[shot_index][row_ids]
        stored = pieces.reshape(N_DOM, 2, DZ, NX, NY).astype(jnp.float32)
        previous = stored[:, 0].reshape(NZ, NX, NY)
        current = stored[:, 1].reshape(NZ, NX, NY)
        forward_laps = []
        for step_num in range(STEPS):
            laplacian = laplace(current)
            forward_laps.append(laplacian)
            if step_num + 1 < STEPS:
                advanced = 2.0 * current - previous + speed_sq * laplacian
                advanced = inject(advanced, src_depth[shot_index:shot_index + 1], src_row[shot_index:shot_index + 1], wavelet[shot_index, step_num:step_num + 1])
                previous, current = current, advanced
        adj_later = adjoint_next[shot_index]
        present = adjoint_now[shot_index]
        summed = jnp.zeros((NZ, NX, NY), jnp.float32)
        for step_num in range(STEPS):
            summed = summed + present * forward_laps[STEPS - 1 - step_num]
            laplacian = laplace(speed_sq * present)
            advanced = 2.0 * present - adj_later + laplacian
            advanced = inject(advanced, rec_depth, rec_row, residuals[shot_index, step_num])
            adj_later, present = present, advanced
        gradient = gradient + grad_scale * summed
        late_list.append(adj_later)
        early_list.append(present)
    return gradient, jnp.stack(late_list), jnp.stack(early_list)
```

```python
import functools

import jax
import jax.numpy as jnp
from jax import lax
from jax.experimental import pallas as pl
from jax.experimental.pallas import tpu as pltpu
from jax.sharding import PartitionSpec as P

STEPS = 4
HALO = 4
PAD = 8

stencil_coef = (-205.0 / 72.0, 8.0 / 5.0, -1.0 / 5.0, 8.0 / 315.0, -1.0 / 560.0)
grad_scale = 0.0625

MESH = pl.DeviceIdType.MESH
F32 = jnp.float32
BF16 = jnp.bfloat16


def split3(value):
    high = value.astype(BF16)
    rest = value - high.astype(F32)
    mid = rest.astype(BF16)
    low = (rest - mid.astype(F32)).astype(BF16)
    return high, mid, low


def window_kernel(
    n_shot,
    n_dom,
    parked,
    slot,
    ints,
    speed_in,
    next_in,
    now_in,
    floats,
    rec_depth,
    rec_row,
    grad_out,
    late_out,
    early_out,
    send_buf,
    recv_buf,
    ints_w,
    ints_s,
    floats_w,
    speed,
    lam_next,
    lam,
    u_first,
    v_buf,
    e_buf,
    lap,
    lap_adj,
    band,
    parts,
    inject,
    src_mask,
    grad_send,
    grad_recv,
    lam_out,
    a2a_send,
    a2a_recv,
    swap_send,
    swap_recv,
    halo_send,
    halo_recv,
    grad_ssem,
    grad_rsem,
    local_sem,
):
    depth, width, lanes = speed_in.shape
    groups = n_shot // 2
    share = width // n_shot
    n_rec = rec_depth.shape[1]
    shot = lax.axis_index("shot")
    dom = lax.axis_index("dom")
    a, c = shot // 2, shot % 2
    b, y = dom // 2, dom % 2
    same = c == y
    my_shot = 2 * a + y
    my_dom = 2 * b + c
    partner = (2 * a + y, 2 * b + c)

    barrier = pltpu.get_barrier_semaphore()

    def greet(shot_to, dom_to):
        pl.semaphore_signal(barrier, inc=1, device_id=(shot_to, dom_to), device_id_type=MESH)

    def greet_dom(i, carry):
        to = (dom + i) % n_dom
        greet(2 * a + c, to)
        greet(2 * a + 1 - c, to)
        return carry

    lax.fori_loop(1, n_dom, greet_dom, 0)
    greet(2 * a + 1 - c, dom)
    for i in range(1, groups):
        other = (a + i) % groups
        for cc in range(2):
            for yy in range(2):
                greet(2 * other + cc, 2 * b + yy)

    pl.semaphore_wait(barrier, 2 * n_dom - 1 + 4 * (groups - 1))

    def remote(src, dst, ssem, rsem, to):
        return pltpu.make_async_remote_copy(
            src_ref=src, dst_ref=dst, send_sem=ssem, recv_sem=rsem, device_id=to, device_id_type=MESH
        )

    def start_to(here, src, dst, ssem, rsem, to):
        @pl.when(here)
        def _():
            pltpu.make_async_copy(src, dst, rsem).start()

        @pl.when(jnp.logical_not(here))
        def _():
            remote(src, dst, ssem, rsem, to).start()

    def wait_sent(here, src, dst, ssem, rsem, to):
        @pl.when(jnp.logical_not(here))
        def _():
            remote(src, dst, ssem, rsem, to).wait_send()

    def wait_got(dst, rsem):
        pltpu.make_async_copy(dst, dst, rsem).wait()

    swaps = [
        (floats, floats_w),
        (ints, ints_w),
        (speed_in, speed),
        (now_in, lam.at[0]),
        (next_in, lam_next),
    ]

    def start_swap(i):
        start_to(same, swaps[i][0], swaps[i][1], swap_send.at[i], swap_recv.at[i], partner)

    def wait_swap(i):
        wait_got(swaps[i][1], swap_recv.at[i])

    start_swap(0)
    start_swap(1)

    def piece_to(o):
        here = jnp.logical_and(same, o == dom)
        return here, (2 * a + o % 2, 2 * (o // 2) + c)

    def send_piece(i, carry):
        o = (dom + i) % n_dom
        here, to = piece_to(o)
        send_buf[o] = parked[slot[o]]
        start_to(here, send_buf.at[o], recv_buf.at[dom], a2a_send.at[o], a2a_recv.at[dom], to)
        return carry

    lax.fori_loop(1, n_dom + 1, send_piece, 0)
    start_swap(2)
    start_swap(3)
    start_swap(4)

    row_i = lax.broadcasted_iota(jnp.int32, (lanes, lanes), 0)
    col_i = lax.broadcasted_iota(jnp.int32, (lanes, lanes), 1)
    apart = jnp.abs(row_i - col_i)
    matrix = jnp.zeros((lanes, lanes), F32)
    for k in range(1, 5):
        matrix = jnp.where(apart == k, stencil_coef[k], matrix)
    m_high, m_mid, m_low = split3(matrix)
    for i, part in enumerate((m_high, m_high, m_high, m_mid, m_mid, m_low)):
        band[i * lanes : (i + 1) * lanes, :] = part
    zeros_pad = jnp.zeros((depth, PAD, lanes), F32)
    for ch in range(2):
        e_buf[ch, :, 0:PAD, :] = zeros_pad
        e_buf[ch, :, PAD + width : 2 * PAD + width, :] = zeros_pad

    has_down = my_dom > 0
    has_up = my_dom < n_dom - 1
    top = 4 + depth

    @pl.when(jnp.logical_not(has_down))
    def _():
        def clear(i, carry):
            v_buf[i // STEPS, i % STEPS, 0:HALO] = jnp.zeros((HALO, width, lanes), F32)
            return carry

        lax.fori_loop(0, 2 * STEPS, clear, 0)

    @pl.when(jnp.logical_not(has_up))
    def _():
        def clear(i, carry):
            v_buf[i // STEPS, i % STEPS, top : top + HALO] = jnp.zeros((HALO, width, lanes), F32)
            return carry

        lax.fori_loop(0, 2 * STEPS, clear, 0)

    local_depth = rec_depth[...] - my_dom * depth
    rec_line = local_depth * width + rec_row[...] // lanes
    rec_lane = rec_row[...] % lanes
    wait_swap(0)
    wait_swap(1)
    to_scalar = pltpu.make_async_copy(ints_w, ints_s, local_sem)
    to_scalar.start()
    lane_hit = lax.broadcasted_iota(jnp.int32, (lanes, n_rec), 0) == rec_lane
    for k in range(STEPS):
        amounts = jnp.where(lane_hit, floats_w[k : k + 1, 0:n_rec], 0.0)
        for i, part in enumerate(split3(amounts)):
            parts[i, k * lanes : (k + 1) * lanes, :] = part
    to_scalar.wait()

    def inject_plane(z, carry):
        line = lax.broadcasted_iota(jnp.int32, (width, n_rec), 0) + z * width
        hit = jnp.where(line == rec_line, 1.0, 0.0).astype(BF16)
        total = jnp.zeros((width, STEPS * lanes), F32)
        for i in range(3):
            total = total + lax.dot_general(
                hit, parts[i], (((1,), (1,)), ((), ())), preferred_element_type=F32
            )
        for k in range(STEPS):
            inject[k, z] = total[:, k * lanes : (k + 1) * lanes]
        return carry

    lax.fori_loop(0, depth, inject_plane, 0)

    src_plane = ints_s[1, 0] - my_dom * depth
    cell = lax.broadcasted_iota(jnp.int32, (width, lanes), 0) * lanes + lax.broadcasted_iota(
        jnp.int32, (width, lanes), 1
    )
    src_mask[...] = jnp.where(cell == ints_s[1, 1], 1.0, 0.0)

    down = (2 * a + (my_dom - 1) % 2, 2 * ((my_dom + 1) // 2 - 1) + y)
    up = (2 * a + (my_dom + 1) % 2, 2 * ((my_dom + 1) // 2) + y)

    def to_down(ch, n):
        i = (ch * STEPS + n) * 2
        v = v_buf.at[ch, n]
        return remote(
            v.at[pl.ds(HALO, HALO)], v.at[pl.ds(top, HALO)], halo_send.at[i], halo_recv.at[i + 1], down
        )

    def to_up(ch, n):
        i = (ch * STEPS + n) * 2
        v = v_buf.at[ch, n]
        return remote(
            v.at[pl.ds(top - HALO, HALO)], v.at[pl.ds(0, HALO)], halo_send.at[i + 1], halo_recv.at[i], up
        )

    def send_down(ch, n):
        @pl.when(has_down)
        def _():
            to_down(ch, n).start()

    def send_up(ch, n):
        @pl.when(has_up)
        def _():
            to_up(ch, n).start()

    def wait_halo(ch, n):
        i = (ch * STEPS + n) * 2
        v = v_buf.at[ch, n]

        @pl.when(has_down)
        def _():
            wait_got(v.at[pl.ds(0, HALO)], halo_recv.at[i])

        @pl.when(has_up)
        def _():
            wait_got(v.at[pl.ds(top, HALO)], halo_recv.at[i + 1])

    def put_field(ch, n, z, value):
        v_buf[ch, n, z + HALO] = value
        e_buf[ch, z, PAD : PAD + width, :] = value

    def lateral(ch, dst):
        def plane(z, carry):
            mid_rows = e_buf[ch, z, PAD : PAD + width, :]
            high, mid, low = split3(mid_rows)
            lhs = jnp.concatenate([high, mid, low, high, mid, high], axis=1)
            total = jnp.dot(lhs, band[...], preferred_element_type=F32)
            total = total + 3.0 * stencil_coef[0] * mid_rows
            for k in range(1, 5):
                total = total + stencil_coef[k] * (
                    e_buf[ch, z, PAD + k : PAD + k + width, :] + e_buf[ch, z, PAD - k : PAD - k + width, :]
                )
            dst[z] = total
            return carry

        lax.fori_loop(0, depth, plane, 0, unroll=2)

    def vertical(ch, n, z):
        total = stencil_coef[1] * (v_buf[ch, n, z + HALO + 1] + v_buf[ch, n, z + HALO - 1])
        for k in range(2, 5):
            total = total + stencil_coef[k] * (v_buf[ch, n, z + HALO + k] + v_buf[ch, n, z + HALO - k])
        return total

    def sweep(body, ch, n):
        lax.fori_loop(0, HALO, body, 0)
        if n is not None:
            send_down(ch, n)
        lax.fori_loop(HALO, depth, body, 0)
        if n is not None:
            send_up(ch, n)

    for h in range(n_dom):
        wait_got(recv_buf.at[h], a2a_recv.at[h])
    rows = recv_buf.shape[1]
    half = n_dom // 2
    per = max(1, rows // width)
    cut = min(rows, width)

    def unpack(p, carry):
        older = recv_buf[ints_s[0, p]].astype(F32)
        newer = recv_buf[ints_s[0, p + half]].astype(F32)
        if rows >= width:
            for j in range(per):
                u_first[p * per + j] = older[j * width : (j + 1) * width]
                put_field(0, 0, p * per + j, newer[j * width : (j + 1) * width])
        else:
            parts_of = width // cut
            z, at = p // parts_of, (p % parts_of) * cut
            at = pl.multiple_of(at, cut)
            u_first[z, pl.ds(at, cut), :] = older
            v_buf[0, 0, z + HALO, pl.ds(at, cut), :] = newer
            e_buf[0, z, pl.ds(at + PAD, cut), :] = newer
        return carry

    lax.fori_loop(0, half, unpack, 0)
    send_down(0, 0)
    send_up(0, 0)
    lateral(0, lap.at[0])

    wait_swap(2)
    wait_swap(3)

    def first_scaled(z, carry):
        put_field(1, 0, z, speed[z] * lam[0, z])
        return carry

    sweep(first_scaled, 1, 0)
    lateral(1, lap_adj)

    def start_late(i, src, dst):
        start_to(same, src, dst, swap_send.at[i], swap_recv.at[i], partner)

    lam_next_ready = False
    for n in range(STEPS):
        wait_halo(0, n)
        last = n == STEPS - 1

        def forward(z, carry, n=n, last=last):
            value = lap[n, z] + vertical(0, n, z)
            lap[n, z] = value
            if not last:
                older = u_first[z] if n == 0 else v_buf[0, n - 1, z + HALO]
                amount = floats_w[n : n + 1, n_rec : n_rec + lanes] * jnp.where(src_plane == z, 1.0, 0.0)
                put_field(
                    0,
                    n + 1,
                    z,
                    2.0 * v_buf[0, n, z + HALO] - older + speed[z] * value + src_mask[...] * amount,
                )
            return carry

        sweep(forward, 0, None if last else n + 1)
        if not last:
            lateral(0, lap.at[n + 1])
        else:

            def gradient(z, carry):
                total = lam[0, z] * lap[STEPS - 1, z]
                for k in range(1, STEPS):
                    total = total + lam[k, z] * lap[STEPS - 1 - k, z]
                total = grad_scale * total
                for j in range(n_shot):
                    grad_send[j, z] = total[j * share : (j + 1) * share]
                return carry

            lax.fori_loop(0, depth, gradient, 0)
            for j in range(n_shot):
                start_to(
                    jnp.logical_and(same, shot == j),
                    grad_send.at[j],
                    grad_recv.at[my_shot],
                    grad_ssem.at[j],
                    grad_rsem.at[my_shot],
                    (j, 2 * b + c),
                )

        if not lam_next_ready:
            wait_swap(4)
            lam_next_ready = True
        wait_halo(1, n)

        def adjoint(z, carry, n=n, last=last):
            older = lam_next[z] if n == 0 else lam[n - 1, z]
            value = 2.0 * lam[n, z] - older + (lap_adj[z] + vertical(1, n, z)) + inject[n, z]
            if last:
                lam_out[z] = value
            else:
                lam[n + 1, z] = value
                put_field(1, n + 1, z, speed[z] * value)
            return carry

        sweep(adjoint, 1, None if last else n + 1)
        if n == STEPS - 2:
            start_late(5, lam.at[STEPS - 1], late_out)
        if last:
            start_late(6, lam_out, early_out)
        else:
            lateral(1, lap_adj)

    for j in range(n_shot):
        wait_got(grad_recv.at[j], grad_rsem.at[j])
    total = grad_recv[0]
    for j in range(1, n_shot):
        total = total + grad_recv[j]
    grad_out[...] = total
    wait_got(late_out, swap_recv.at[5])
    wait_got(early_out, swap_recv.at[6])

    for i, (src, dst) in enumerate(swaps + [(lam.at[STEPS - 1], late_out), (lam_out, early_out)]):
        wait_sent(same, src, dst, swap_send.at[i], swap_recv.at[i], partner)

    def piece_sent(o, carry):
        here, to = piece_to(o)
        wait_sent(here, send_buf.at[o], recv_buf.at[dom], a2a_send.at[o], a2a_recv.at[dom], to)
        return carry

    lax.fori_loop(0, n_dom, piece_sent, 0)
    for j in range(n_shot):
        wait_sent(
            jnp.logical_and(same, shot == j),
            grad_send.at[j],
            grad_recv.at[my_shot],
            grad_ssem.at[j],
            grad_rsem.at[my_shot],
            (j, 2 * b + c),
        )

    @pl.when(has_down)
    def _():
        for ch in range(2):
            for n in range(STEPS):
                to_down(ch, n).wait_send()

    @pl.when(has_up)
    def _():
        for ch in range(2):
            for n in range(STEPS):
                to_up(ch, n).wait_send()


def per_device(
    n_shot,
    n_dom,
    parked,
    parked_slot,
    holder_list,
    speed_sq,
    adjoint_next,
    adjoint_now,
    wavelet,
    src_depth,
    src_row,
    rec_depth,
    rec_row,
    residuals,
):
    depth, width, lanes = speed_sq.shape
    n_rec = rec_depth.shape[0]
    piece = parked.shape[2]
    rows = piece // lanes
    pieces = parked[0].reshape(n_dom, rows, lanes)
    ints = jnp.concatenate(
        [
            jnp.pad(holder_list[0], ((0, 0), (0, 128 - n_dom))),
            jnp.pad(jnp.concatenate([src_depth, src_row])[None], ((0, 6), (0, 126))),
        ],
        axis=0,
    )
    floats = jnp.concatenate(
        [
            jnp.pad(residuals[0], ((0, 8 - STEPS), (0, 0))),
            jnp.broadcast_to(
                jnp.pad(wavelet[0], (0, 8 - (STEPS - 1)))[:, None], (8, lanes)
            ),
        ],
        axis=1,
    )
    vmem = pl.BlockSpec(memory_space=pltpu.VMEM)
    smem = pl.BlockSpec(memory_space=pltpu.SMEM)
    slab = (depth, width, lanes)
    dma = pltpu.SemaphoreType.DMA
    share = width // n_shot
    grad, late, early = pl.pallas_call(
        functools.partial(window_kernel, n_shot, n_dom),
        out_shape=[
            jax.ShapeDtypeStruct((depth, share, lanes), F32),
            jax.ShapeDtypeStruct(slab, F32),
            jax.ShapeDtypeStruct(slab, F32),
        ],
        in_specs=[vmem, smem] + [vmem] * 7,
        out_specs=[vmem] * 3,
        scratch_shapes=[
            pltpu.VMEM((n_dom, rows, lanes), BF16),
            pltpu.VMEM((n_dom, rows, lanes), BF16),
            pltpu.VMEM((8, 128), jnp.int32),
            pltpu.SMEM((8, 128), jnp.int32),
            pltpu.VMEM((8, n_rec + lanes), F32),
            pltpu.VMEM(slab, F32),
            pltpu.VMEM(slab, F32),
            pltpu.VMEM((STEPS,) + slab, F32),
            pltpu.VMEM(slab, F32),
            pltpu.VMEM((2, STEPS, depth + 2 * HALO, width, lanes), F32),
            pltpu.VMEM((2, depth, width + 2 * PAD, lanes), F32),
            pltpu.VMEM((STEPS,) + slab, F32),
            pltpu.VMEM(slab, F32),
            pltpu.VMEM((6 * lanes, lanes), BF16),
            pltpu.VMEM((3, STEPS * lanes, n_rec), BF16),
            pltpu.VMEM((STEPS,) + slab, F32),
            pltpu.VMEM((width, lanes), F32),
            pltpu.VMEM((n_shot, depth, share, lanes), F32),
            pltpu.VMEM((n_shot, depth, share, lanes), F32),
            pltpu.VMEM(slab, F32),
            dma((n_dom,)),
            dma((n_dom,)),
            dma((7,)),
            dma((7,)),
            dma((4 * STEPS,)),
            dma((4 * STEPS,)),
            dma((n_shot,)),
            dma((n_shot,)),
            dma,
        ],
        compiler_params=pltpu.CompilerParams(
            collective_id=0, has_side_effects=True, vmem_limit_bytes=48 * 1024 * 1024
        ),
        name="adjoint_window",
    )(
        pieces,
        parked_slot[0, 0],
        ints,
        speed_sq,
        adjoint_next[0],
        adjoint_now[0],
        floats,
        rec_depth[None],
        rec_row[None],
    )
    return grad, late[None], early[None]


def solution(mesh):
    n_shot, n_dom = mesh.shape["shot"], mesh.shape["dom"]
    in_specs = (
        P("shot", "dom", None),
        P("shot", "dom", None),
        P("shot", "dom", None),
        P("dom", None, None),
        P("shot", "dom", None, None),
        P("shot", "dom", None, None),
        P("shot", None),
        P("shot"),
        P("shot"),
        P(),
        P(),
        P("shot", None, None),
    )
    out_specs = (P("dom", "shot", None), P("shot", "dom", None, None), P("shot", "dom", None, None))
    return jax.shard_map(
        functools.partial(per_device, n_shot, n_dom),
        mesh=mesh,
        in_specs=in_specs,
        out_specs=out_specs,
        check_vma=False,
    )
```

```python
import functools

import jax
import jax.numpy as jnp
from jax import lax
from jax.experimental import pallas as pl
from jax.experimental.pallas import tpu as pltpu
from jax.sharding import PartitionSpec as P

STEPS = 4
HALO = 4
PAD = 8
VMEM_BYTES = 56 * 1024 * 1024

stencil_coef = (-205.0 / 72.0, 8.0 / 5.0, -1.0 / 5.0, 8.0 / 315.0, -1.0 / 560.0)
grad_scale = 0.0625

MESH = pl.DeviceIdType.MESH
F32 = jnp.float32
BF16 = jnp.bfloat16


def split3(value):
    high = value.astype(BF16)
    rest = value - high.astype(F32)
    mid = rest.astype(BF16)
    low = (rest - mid.astype(F32)).astype(BF16)
    return high, mid, low


def window_kernel(
    n_shot,
    n_dom,
    parked,
    slot,
    ints,
    speed_in,
    next_in,
    now_in,
    floats,
    rec_depth,
    rec_row,
    grad_out,
    late_out,
    early_out,
    send_buf,
    recv_buf,
    ints_w,
    ints_s,
    floats_w,
    speed,
    lam_next,
    lam,
    u_first,
    v_buf,
    e_buf,
    lap,
    lap_adj,
    band,
    parts,
    inject,
    src_mask,
    grad_send,
    grad_recv,
    lam_out,
    lap_w,
    grad_part,
    grad_part_w,
    a2a_send,
    a2a_recv,
    swap_send,
    swap_recv,
    halo_send,
    halo_recv,
    grad_ssem,
    grad_rsem,
    local_sem,
):
    depth, width, lanes = speed_in.shape
    groups = n_shot // 2
    share = width // n_shot
    n_rec = rec_depth.shape[1]
    shot = lax.axis_index("shot")
    dom = lax.axis_index("dom")
    a, c = shot // 2, shot % 2
    b, y = dom // 2, dom % 2
    same = c == y
    my_dom = 2 * b + c
    partner = (2 * a + y, 2 * b + c)

    barrier = pltpu.get_barrier_semaphore()

    def greet(shot_to, dom_to):
        pl.semaphore_signal(barrier, inc=1, device_id=(shot_to, dom_to), device_id_type=MESH)

    def greet_dom(i, carry):
        to = (dom + i) % n_dom
        greet(2 * a + c, to)
        greet(2 * a + 1 - c, to)
        return carry

    lax.fori_loop(1, n_dom, greet_dom, 0)
    greet(2 * a + 1 - c, dom)
    for i in range(1, groups):
        other = (a + i) % groups
        for cc in range(2):
            for yy in range(2):
                greet(2 * other + cc, 2 * b + yy)

    pl.semaphore_wait(barrier, 2 * n_dom - 1 + 4 * (groups - 1))

    def remote(src, dst, ssem, rsem, to):
        return pltpu.make_async_remote_copy(
            src_ref=src, dst_ref=dst, send_sem=ssem, recv_sem=rsem, device_id=to, device_id_type=MESH
        )

    def start_to(here, src, dst, ssem, rsem, to):
        @pl.when(here)
        def _():
            pltpu.make_async_copy(src, dst, rsem).start()

        @pl.when(jnp.logical_not(here))
        def _():
            remote(src, dst, ssem, rsem, to).start()

    def wait_sent(here, src, dst, ssem, rsem, to):
        @pl.when(jnp.logical_not(here))
        def _():
            remote(src, dst, ssem, rsem, to).wait_send()

    def wait_got(dst, rsem):
        pltpu.make_async_copy(dst, dst, rsem).wait()

    swaps = [
        (floats, floats_w),
        (ints, ints_w),
        (speed_in, speed),
        (now_in, lam.at[0]),
        (next_in, lam_next),
        (lam.at[STEPS - 1], late_out),
        (lam_out, early_out),
        (lap.at[0], lap_w),
        (grad_part, grad_part_w),
    ]

    def start_swap(i):
        start_to(same, swaps[i][0], swaps[i][1], swap_send.at[i], swap_recv.at[i], partner)

    def wait_swap(i):
        wait_got(swaps[i][1], swap_recv.at[i])

    start_swap(0)
    start_swap(1)

    def piece_to(o):
        here = jnp.logical_and(same, o == dom)
        return here, (2 * a + o % 2, 2 * (o // 2) + c)

    def send_piece(i, carry):
        o = (dom + i) % n_dom
        here, to = piece_to(o)
        send_buf[o] = parked[slot[o]]
        start_to(here, send_buf.at[o], recv_buf.at[dom], a2a_send.at[o], a2a_recv.at[dom], to)
        return carry

    lax.fori_loop(1, n_dom + 1, send_piece, 0)
    start_swap(2)
    start_swap(3)
    start_swap(4)

    row_i = lax.broadcasted_iota(jnp.int32, (lanes, lanes), 0)
    col_i = lax.broadcasted_iota(jnp.int32, (lanes, lanes), 1)
    apart = jnp.abs(row_i - col_i)
    matrix = jnp.zeros((lanes, lanes), F32)
    for k in range(1, 5):
        matrix = jnp.where(apart == k, stencil_coef[k], matrix)
    m_high, m_mid, m_low = split3(matrix)
    for i, part in enumerate((m_high, m_high, m_high, m_mid, m_mid, m_low)):
        band[i * lanes : (i + 1) * lanes, :] = part
    zeros_pad = jnp.zeros((depth, PAD, lanes), F32)
    for ch in range(2):
        e_buf[ch, :, 0:PAD, :] = zeros_pad
        e_buf[ch, :, PAD + width : 2 * PAD + width, :] = zeros_pad

    has_down = my_dom > 0
    has_up = my_dom < n_dom - 1
    top = 4 + depth

    @pl.when(jnp.logical_not(has_down))
    def _():
        def clear(i, carry):
            v_buf[i // STEPS, i % STEPS, 0:HALO] = jnp.zeros((HALO, width, lanes), F32)
            return carry

        lax.fori_loop(0, 2 * STEPS, clear, 0)

    @pl.when(jnp.logical_not(has_up))
    def _():
        def clear(i, carry):
            v_buf[i // STEPS, i % STEPS, top : top + HALO] = jnp.zeros((HALO, width, lanes), F32)
            return carry

        lax.fori_loop(0, 2 * STEPS, clear, 0)

    local_depth = rec_depth[...] - my_dom * depth
    rec_line = local_depth * width + rec_row[...] // lanes
    rec_lane = rec_row[...] % lanes
    wait_swap(0)
    wait_swap(1)
    to_scalar = pltpu.make_async_copy(ints_w, ints_s, local_sem)
    to_scalar.start()
    lane_hit = lax.broadcasted_iota(jnp.int32, (lanes, n_rec), 0) == rec_lane
    for k in range(STEPS):
        amounts = jnp.where(lane_hit, floats_w[k : k + 1, 0:n_rec], 0.0)
        for i, part in enumerate(split3(amounts)):
            parts[i, k * lanes : (k + 1) * lanes, :] = part
    to_scalar.wait()

    def inject_plane(z, carry):
        line = lax.broadcasted_iota(jnp.int32, (width, n_rec), 0) + z * width
        hit = jnp.where(line == rec_line, 1.0, 0.0).astype(BF16)
        total = jnp.zeros((width, STEPS * lanes), F32)
        for i in range(3):
            total = total + lax.dot_general(
                hit, parts[i], (((1,), (1,)), ((), ())), preferred_element_type=F32
            )
        for k in range(STEPS):
            inject[k, z] = total[:, k * lanes : (k + 1) * lanes]
        return carry

    lax.fori_loop(0, depth, inject_plane, 0)

    src_plane = ints_s[1, 0] - my_dom * depth
    cell = lax.broadcasted_iota(jnp.int32, (width, lanes), 0) * lanes + lax.broadcasted_iota(
        jnp.int32, (width, lanes), 1
    )
    src_mask[...] = jnp.where(cell == ints_s[1, 1], 1.0, 0.0)

    down = (2 * a + (my_dom - 1) % 2, 2 * ((my_dom + 1) // 2 - 1) + y)
    up = (2 * a + (my_dom + 1) % 2, 2 * ((my_dom + 1) // 2) + y)

    def to_down(ch, n):
        i = (ch * STEPS + n) * 2
        v = v_buf.at[ch, n]
        return remote(
            v.at[pl.ds(HALO, HALO)], v.at[pl.ds(top, HALO)], halo_send.at[i], halo_recv.at[i + 1], down
        )

    def to_up(ch, n):
        i = (ch * STEPS + n) * 2
        v = v_buf.at[ch, n]
        return remote(
            v.at[pl.ds(top - HALO, HALO)], v.at[pl.ds(0, HALO)], halo_send.at[i + 1], halo_recv.at[i], up
        )

    def send_down(ch, n):
        @pl.when(has_down)
        def _():
            to_down(ch, n).start()

    def send_up(ch, n):
        @pl.when(has_up)
        def _():
            to_up(ch, n).start()

    def wait_halo(ch, n):
        i = (ch * STEPS + n) * 2
        v = v_buf.at[ch, n]

        @pl.when(has_down)
        def _():
            wait_got(v.at[pl.ds(0, HALO)], halo_recv.at[i])

        @pl.when(has_up)
        def _():
            wait_got(v.at[pl.ds(top, HALO)], halo_recv.at[i + 1])

    def put_field(ch, n, z, value):
        v_buf[ch, n, z + HALO] = value
        e_buf[ch, z, PAD : PAD + width, :] = value

    def lateral(ch, dst):
        def plane(z, carry):
            mid_rows = e_buf[ch, z, PAD : PAD + width, :]
            high, mid, low = split3(mid_rows)
            lhs = jnp.concatenate([high, mid, low, high, mid, high], axis=1)
            total = jnp.dot(lhs, band[...], preferred_element_type=F32)
            total = total + 3.0 * stencil_coef[0] * mid_rows
            for k in range(1, 5):
                total = total + stencil_coef[k] * (
                    e_buf[ch, z, PAD + k : PAD + k + width, :] + e_buf[ch, z, PAD - k : PAD - k + width, :]
                )
            dst[z] = total
            return carry

        lax.fori_loop(0, depth, plane, 0, unroll=2)

    def vertical(ch, n, z):
        total = stencil_coef[1] * (v_buf[ch, n, z + HALO + 1] + v_buf[ch, n, z + HALO - 1])
        for k in range(2, 5):
            total = total + stencil_coef[k] * (v_buf[ch, n, z + HALO + k] + v_buf[ch, n, z + HALO - k])
        return total

    def sweep(body, ch, n):
        lax.fori_loop(0, HALO, body, 0)
        if n is not None:
            send_down(ch, n)
        lax.fori_loop(HALO, depth, body, 0)
        if n is not None:
            send_up(ch, n)

    for h in range(n_dom):
        wait_got(recv_buf.at[h], a2a_recv.at[h])
    rows = recv_buf.shape[1]
    half = n_dom // 2
    per = max(1, rows // width)
    cut = min(rows, width)

    def unpack(p, carry):
        older = recv_buf[ints_s[0, p]].astype(F32)
        newer = recv_buf[ints_s[0, p + half]].astype(F32)
        if rows >= width:
            for j in range(per):
                u_first[p * per + j] = older[j * width : (j + 1) * width]
                put_field(0, 0, p * per + j, newer[j * width : (j + 1) * width])
        else:
            parts_of = width // cut
            z, at = p // parts_of, (p % parts_of) * cut
            at = pl.multiple_of(at, cut)
            u_first[z, pl.ds(at, cut), :] = older
            v_buf[0, 0, z + HALO, pl.ds(at, cut), :] = newer
            e_buf[0, z, pl.ds(at + PAD, cut), :] = newer
        return carry

    lax.fori_loop(0, half, unpack, 0)
    send_down(0, 0)
    send_up(0, 0)
    lateral(0, lap.at[0])

    def forward_step(n):
        last = n == STEPS - 1
        wait_halo(0, n)

        def plane(z, carry):
            value = lap[n, z] + vertical(0, n, z)
            lap[n, z] = value
            if not last:
                older = u_first[z] if n == 0 else v_buf[0, n - 1, z + HALO]
                amount = floats_w[n : n + 1, n_rec : n_rec + lanes] * jnp.where(src_plane == z, 1.0, 0.0)
                put_field(
                    0,
                    n + 1,
                    z,
                    2.0 * v_buf[0, n, z + HALO] - older + speed[z] * value + src_mask[...] * amount,
                )
            return carry

        sweep(plane, 0, None if last else n + 1)
        if not last:
            lateral(0, lap.at[n + 1])

    def adjoint_step(n):
        last = n == STEPS - 1
        wait_halo(1, n)

        def plane(z, carry):
            older = lam_next[z] if n == 0 else lam[n - 1, z]
            value = 2.0 * lam[n, z] - older + (lap_adj[z] + vertical(1, n, z)) + inject[n, z]
            if last:
                lam_out[z] = value
            else:
                lam[n + 1, z] = value
                put_field(1, n + 1, z, speed[z] * value)
            return carry

        sweep(plane, 1, None if last else n + 1)

    wait_swap(2)
    forward_step(0)
    wait_swap(3)

    def first_scaled(z, carry):
        put_field(1, 0, z, speed[z] * lam[0, z])
        return carry

    sweep(first_scaled, 1, 0)
    lateral(1, lap_adj)
    forward_step(1)
    wait_swap(4)
    start_swap(7)
    adjoint_step(0)
    lateral(1, lap_adj)
    forward_step(2)
    adjoint_step(1)
    lateral(1, lap_adj)
    forward_step(3)

    def early_terms(z, carry):
        total = lam[0, z] * lap[STEPS - 1, z]
        for k in range(1, STEPS - 1):
            total = total + lam[k, z] * lap[STEPS - 1 - k, z]
        grad_part[z] = total
        return carry

    lax.fori_loop(0, depth, early_terms, 0)
    start_swap(8)
    adjoint_step(2)
    start_swap(5)
    lateral(1, lap_adj)
    adjoint_step(3)
    start_swap(6)

    wait_swap(7)
    wait_swap(8)
    wait_swap(5)

    def gradient(z, carry):
        total = grad_scale * (grad_part_w[z] + late_out[z] * lap_w[z])
        for j in range(n_shot):
            grad_send[j, z] = total[j * share : (j + 1) * share]
        return carry

    lax.fori_loop(0, depth, gradient, 0)

    def share_to(i):
        j = (shot + i) % n_shot
        return remote(grad_send.at[j], grad_recv.at[shot], grad_ssem.at[j], grad_rsem.at[shot], (j, dom))

    for i in range(1, n_shot):
        share_to(i).start()
    total = grad_send[shot]
    for i in range(1, n_shot):
        j = (shot + i) % n_shot
        wait_got(grad_recv.at[j], grad_rsem.at[j])
        total = total + grad_recv[j]
    grad_out[...] = total
    wait_swap(6)

    for i, (src, dst) in enumerate(swaps):
        wait_sent(same, src, dst, swap_send.at[i], swap_recv.at[i], partner)

    def piece_sent(o, carry):
        here, to = piece_to(o)
        wait_sent(here, send_buf.at[o], recv_buf.at[dom], a2a_send.at[o], a2a_recv.at[dom], to)
        return carry

    lax.fori_loop(0, n_dom, piece_sent, 0)
    for i in range(1, n_shot):
        share_to(i).wait_send()

    @pl.when(has_down)
    def _():
        for ch in range(2):
            for n in range(STEPS):
                to_down(ch, n).wait_send()

    @pl.when(has_up)
    def _():
        for ch in range(2):
            for n in range(STEPS):
                to_up(ch, n).wait_send()


def hand_on(*refs):
    sems = refs[6]
    copies = [pltpu.make_async_copy(refs[i], refs[3 + i], sems.at[i]) for i in range(3)]
    for copy in copies:
        copy.start()
    for copy in copies:
        copy.wait()


def per_device(
    n_shot,
    n_dom,
    parked,
    parked_slot,
    holder_list,
    speed_sq,
    adjoint_next,
    adjoint_now,
    wavelet,
    src_depth,
    src_row,
    rec_depth,
    rec_row,
    residuals,
):
    depth, width, lanes = speed_sq.shape
    n_rec = rec_depth.shape[0]
    piece = parked.shape[2]
    rows = piece // lanes
    pieces = parked[0].reshape(n_dom, rows, lanes)
    ints = jnp.concatenate(
        [
            jnp.pad(holder_list[0], ((0, 0), (0, 128 - n_dom))),
            jnp.pad(jnp.concatenate([src_depth, src_row])[None], ((0, 6), (0, 126))),
        ],
        axis=0,
    )
    floats = jnp.concatenate(
        [
            jnp.pad(residuals[0], ((0, 8 - STEPS), (0, 0))),
            jnp.broadcast_to(
                jnp.pad(wavelet[0], (0, 8 - (STEPS - 1)))[:, None], (8, lanes)
            ),
        ],
        axis=1,
    )
    vmem = pl.BlockSpec(memory_space=pltpu.VMEM)
    smem = pl.BlockSpec(memory_space=pltpu.SMEM)
    anywhere = pl.BlockSpec(memory_space=pl.ANY)
    slab = (depth, width, lanes)
    dma = pltpu.SemaphoreType.DMA
    share = width // n_shot
    grad, late, early = pl.pallas_call(
        functools.partial(window_kernel, n_shot, n_dom),
        out_shape=[
            jax.ShapeDtypeStruct((depth, share, lanes), F32),
            jax.ShapeDtypeStruct(slab, F32),
            jax.ShapeDtypeStruct(slab, F32),
        ],
        in_specs=[vmem, smem, vmem, anywhere, anywhere, anywhere] + [vmem] * 3,
        out_specs=[vmem] * 3,
        scratch_shapes=[
            pltpu.VMEM((n_dom, rows, lanes), BF16),
            pltpu.VMEM((n_dom, rows, lanes), BF16),
            pltpu.VMEM((8, 128), jnp.int32),
            pltpu.SMEM((8, 128), jnp.int32),
            pltpu.VMEM((8, n_rec + lanes), F32),
            pltpu.VMEM(slab, F32),
            pltpu.VMEM(slab, F32),
            pltpu.VMEM((STEPS,) + slab, F32),
            pltpu.VMEM(slab, F32),
            pltpu.VMEM((2, STEPS, depth + 2 * HALO, width, lanes), F32),
            pltpu.VMEM((2, depth, width + 2 * PAD, lanes), F32),
            pltpu.VMEM((STEPS,) + slab, F32),
            pltpu.VMEM(slab, F32),
            pltpu.VMEM((6 * lanes, lanes), BF16),
            pltpu.VMEM((3, STEPS * lanes, n_rec), BF16),
            pltpu.VMEM((STEPS,) + slab, F32),
            pltpu.VMEM((width, lanes), F32),
            pltpu.VMEM((n_shot, depth, share, lanes), F32),
            pltpu.VMEM((n_shot, depth, share, lanes), F32),
            pltpu.VMEM(slab, F32),
            pltpu.VMEM(slab, F32),
            pltpu.VMEM(slab, F32),
            pltpu.VMEM(slab, F32),
            dma((n_dom,)),
            dma((n_dom,)),
            dma((9,)),
            dma((9,)),
            dma((4 * STEPS,)),
            dma((4 * STEPS,)),
            dma((n_shot,)),
            dma((n_shot,)),
            dma,
        ],
        compiler_params=pltpu.CompilerParams(
            collective_id=0, has_side_effects=True, vmem_limit_bytes=VMEM_BYTES
        ),
        name="adjoint_window",
    )(
        pieces,
        parked_slot[0, 0],
        ints,
        speed_sq,
        adjoint_next[0],
        adjoint_now[0],
        floats,
        rec_depth[None],
        rec_row[None],
    )
    outs = (grad, late, early)
    grad, late, early = pl.pallas_call(
        hand_on,
        out_shape=[jax.ShapeDtypeStruct(x.shape, x.dtype) for x in outs],
        in_specs=[anywhere] * 3,
        out_specs=[anywhere] * 3,
        scratch_shapes=[dma((3,))],
        name="hand_on",
    )(*outs)
    return grad, late[None], early[None]


def solution(mesh):
    n_shot, n_dom = mesh.shape["shot"], mesh.shape["dom"]
    in_specs = (
        P("shot", "dom", None),
        P("shot", "dom", None),
        P("shot", "dom", None),
        P("dom", None, None),
        P("shot", "dom", None, None),
        P("shot", "dom", None, None),
        P("shot", None),
        P("shot"),
        P("shot"),
        P(),
        P(),
        P("shot", None, None),
    )
    out_specs = (P("dom", "shot", None), P("shot", "dom", None, None), P("shot", "dom", None, None))
    return jax.shard_map(
        functools.partial(per_device, n_shot, n_dom),
        mesh=mesh,
        in_specs=in_specs,
        out_specs=out_specs,
        check_vma=False,
    )
```

```python
import functools

import jax
import jax.numpy as jnp
from jax import lax
from jax.experimental import pallas as pl
from jax.experimental.pallas import tpu as pltpu
from jax.sharding import PartitionSpec as P

STEPS = 4
HALO = 4
PAD = 8
VMEM_BYTES = 56 * 1024 * 1024

stencil_coef = (-205.0 / 72.0, 8.0 / 5.0, -1.0 / 5.0, 8.0 / 315.0, -1.0 / 560.0)
grad_scale = 0.0625

MESH = pl.DeviceIdType.MESH
F32 = jnp.float32
BF16 = jnp.bfloat16


def split2(value):
    high = value.astype(BF16)
    return high, (value - high.astype(F32)).astype(BF16)


def window_kernel(
    n_shot,
    n_dom,
    parked,
    slot,
    holder,
    wavelet,
    src_depth,
    src_row,
    residuals,
    speed_in,
    next_in,
    now_in,
    rec_depth,
    rec_row,
    grad_out,
    late_out,
    early_out,
    send_buf,
    recv_buf,
    ints,
    floats,
    ints_w,
    ints_s,
    floats_w,
    speed,
    lam_next,
    lam,
    u_first,
    v_buf,
    e_buf,
    lap,
    lap_adj,
    band,
    parts,
    inject,
    src_mask,
    grad_send,
    grad_recv,
    lam_out,
    lap_w,
    grad_part,
    grad_part_w,
    a2a_send,
    a2a_recv,
    swap_send,
    swap_recv,
    halo_send,
    halo_recv,
    grad_ssem,
    grad_rsem,
    local_sem,
):
    depth, width, lanes = speed_in.shape
    groups = n_shot // 2
    share = width // n_shot
    n_rec = rec_depth.shape[1]
    shot = lax.axis_index("shot")
    dom = lax.axis_index("dom")
    a, c = shot // 2, shot % 2
    b, y = dom // 2, dom % 2
    same = c == y
    my_dom = 2 * b + c
    partner = (2 * a + y, 2 * b + c)

    lane = lax.broadcasted_iota(jnp.int32, (8, 128), 1)
    line = lax.broadcasted_iota(jnp.int32, (8, 128), 0)
    first = lax.fori_loop(
        0, n_dom, lambda p, v: jnp.where(lane == p, holder[p], v), jnp.zeros((8, 128), jnp.int32)
    )
    second = jnp.where(lane == 0, src_depth[0], src_row[0])
    ints[...] = jnp.where(line == 0, first, second)
    floats[0:STEPS, 0:n_rec] = residuals[...]
    for n in range(STEPS - 1):
        floats[n : n + 1, n_rec : n_rec + lanes] = jnp.full((1, lanes), wavelet[n], F32)
    floats[STEPS - 1 : STEPS, n_rec : n_rec + lanes] = jnp.zeros((1, lanes), F32)
    floats[STEPS:8, :] = jnp.zeros((8 - STEPS, n_rec + lanes), F32)

    barrier = pltpu.get_barrier_semaphore()

    def greet(shot_to, dom_to):
        pl.semaphore_signal(barrier, inc=1, device_id=(shot_to, dom_to), device_id_type=MESH)

    def greet_dom(i, carry):
        to = (dom + i) % n_dom
        greet(2 * a + c, to)
        greet(2 * a + 1 - c, to)
        return carry

    lax.fori_loop(1, n_dom, greet_dom, 0)
    greet(2 * a + 1 - c, dom)
    for i in range(1, groups):
        other = (a + i) % groups
        for cc in range(2):
            for yy in range(2):
                greet(2 * other + cc, 2 * b + yy)

    pl.semaphore_wait(barrier, 2 * n_dom - 1 + 4 * (groups - 1))

    def remote(src, dst, ssem, rsem, to):
        return pltpu.make_async_remote_copy(
            src_ref=src, dst_ref=dst, send_sem=ssem, recv_sem=rsem, device_id=to, device_id_type=MESH
        )

    def start_to(here, src, dst, ssem, rsem, to):
        @pl.when(here)
        def _():
            pltpu.make_async_copy(src, dst, rsem).start()

        @pl.when(jnp.logical_not(here))
        def _():
            remote(src, dst, ssem, rsem, to).start()

    def wait_sent(here, src, dst, ssem, rsem, to):
        @pl.when(jnp.logical_not(here))
        def _():
            remote(src, dst, ssem, rsem, to).wait_send()

    def wait_got(dst, rsem):
        pltpu.make_async_copy(dst, dst, rsem).wait()

    swaps = [
        (floats, floats_w),
        (ints, ints_w),
        (speed_in, speed),
        (now_in, lam.at[0]),
        (next_in, lam_next),
        (lam.at[STEPS - 1], late_out),
        (lam_out, early_out),
        (lap.at[0], lap_w),
        (grad_part, grad_part_w),
    ]

    def start_swap(i):
        start_to(same, swaps[i][0], swaps[i][1], swap_send.at[i], swap_recv.at[i], partner)

    def wait_swap(i):
        wait_got(swaps[i][1], swap_recv.at[i])

    start_swap(0)
    start_swap(1)

    def piece_to(o):
        here = jnp.logical_and(same, o == dom)
        return here, (2 * a + o % 2, 2 * (o // 2) + c)

    def send_piece(i, carry):
        o = (dom + i) % n_dom
        here, to = piece_to(o)
        send_buf[o] = parked[slot[o]]
        start_to(here, send_buf.at[o], recv_buf.at[dom], a2a_send.at[o], a2a_recv.at[dom], to)
        return carry

    lax.fori_loop(1, n_dom + 1, send_piece, 0)
    start_swap(2)

    row_i = lax.broadcasted_iota(jnp.int32, (lanes, lanes), 0)
    col_i = lax.broadcasted_iota(jnp.int32, (lanes, lanes), 1)
    apart = jnp.abs(row_i - col_i)
    matrix = jnp.zeros((lanes, lanes), F32)
    for k in range(1, 5):
        matrix = jnp.where(apart == k, stencil_coef[k], matrix)
    m_high, m_low = split2(matrix)
    for i, part in enumerate((m_high, m_high, m_low, m_low)):
        band[i * lanes : (i + 1) * lanes, :] = part
    zeros_pad = jnp.zeros((depth, PAD, lanes), F32)
    for ch in range(2):
        e_buf[ch, :, 0:PAD, :] = zeros_pad
        e_buf[ch, :, PAD + width : 2 * PAD + width, :] = zeros_pad

    has_down = my_dom > 0
    has_up = my_dom < n_dom - 1
    top = 4 + depth

    @pl.when(jnp.logical_not(has_down))
    def _():
        def clear(i, carry):
            v_buf[i // STEPS, i % STEPS, 0:HALO] = jnp.zeros((HALO, width, lanes), F32)
            return carry

        lax.fori_loop(0, 2 * STEPS, clear, 0)

    @pl.when(jnp.logical_not(has_up))
    def _():
        def clear(i, carry):
            v_buf[i // STEPS, i % STEPS, top : top + HALO] = jnp.zeros((HALO, width, lanes), F32)
            return carry

        lax.fori_loop(0, 2 * STEPS, clear, 0)

    local_depth = rec_depth[...] - my_dom * depth
    rec_line = local_depth * width + rec_row[...] // lanes
    rec_lane = rec_row[...] % lanes
    wait_swap(0)
    wait_swap(1)
    to_scalar = pltpu.make_async_copy(ints_w, ints_s, local_sem)
    to_scalar.start()
    lane_hit = lax.broadcasted_iota(jnp.int32, (lanes, n_rec), 0) == rec_lane
    for k in range(STEPS):
        amounts = jnp.where(lane_hit, floats_w[k : k + 1, 0:n_rec], 0.0)
        for i, part in enumerate(split2(amounts)):
            parts[i, k * lanes : (k + 1) * lanes, :] = part
    to_scalar.wait()

    group = depth // 2

    def inject_half(h, carry):
        line = lax.broadcasted_iota(jnp.int32, (group * width, n_rec), 0) + h * (group * width)
        hit = jnp.where(line == rec_line, 1.0, 0.0).astype(BF16)
        total = jnp.zeros((group * width, STEPS * lanes), F32)
        for i in range(2):
            total = total + lax.dot_general(
                hit, parts[i], (((1,), (1,)), ((), ())), preferred_element_type=F32
            )
        for k in range(STEPS):
            for z in range(group):
                inject[k, h * group + z] = total[z * width : (z + 1) * width, k * lanes : (k + 1) * lanes]
        return carry

    lax.fori_loop(0, 2, inject_half, 0)

    start_swap(3)
    src_plane = ints_s[1, 0] - my_dom * depth
    cell = lax.broadcasted_iota(jnp.int32, (width, lanes), 0) * lanes + lax.broadcasted_iota(
        jnp.int32, (width, lanes), 1
    )
    src_mask[...] = jnp.where(cell == ints_s[1, 1], 1.0, 0.0)

    down = (2 * a + (my_dom - 1) % 2, 2 * ((my_dom + 1) // 2 - 1) + y)
    up = (2 * a + (my_dom + 1) % 2, 2 * ((my_dom + 1) // 2) + y)

    def to_down(ch, n):
        i = (ch * STEPS + n) * 2
        v = v_buf.at[ch, n]
        return remote(
            v.at[pl.ds(HALO, HALO)], v.at[pl.ds(top, HALO)], halo_send.at[i], halo_recv.at[i + 1], down
        )

    def to_up(ch, n):
        i = (ch * STEPS + n) * 2
        v = v_buf.at[ch, n]
        return remote(
            v.at[pl.ds(top - HALO, HALO)], v.at[pl.ds(0, HALO)], halo_send.at[i + 1], halo_recv.at[i], up
        )

    def send_down(ch, n):
        @pl.when(has_down)
        def _():
            to_down(ch, n).start()

    def send_up(ch, n):
        @pl.when(has_up)
        def _():
            to_up(ch, n).start()

    def wait_halo(ch, n):
        i = (ch * STEPS + n) * 2
        v = v_buf.at[ch, n]

        @pl.when(has_down)
        def _():
            wait_got(v.at[pl.ds(0, HALO)], halo_recv.at[i])

        @pl.when(has_up)
        def _():
            wait_got(v.at[pl.ds(top, HALO)], halo_recv.at[i + 1])

    def put_field(ch, n, z, value):
        v_buf[ch, n, z + HALO] = value
        e_buf[ch, z, PAD : PAD + width, :] = value

    def lateral(ch, dst):
        def planes(h, carry):
            z = h * group
            own = e_buf[ch, pl.ds(z, group), PAD : PAD + width, :]
            high, low = split2(own.reshape(group * width, lanes))
            total = jnp.dot(
                jnp.concatenate([high, low, high, low], axis=1), band[...], preferred_element_type=F32
            ).reshape(group, width, lanes)
            for p in range(group):
                value = total[p] + 3.0 * stencil_coef[0] * own[p]
                for k in range(1, 5):
                    value = value + stencil_coef[k] * (
                        e_buf[ch, z + p, PAD + k : PAD + k + width, :]
                        + e_buf[ch, z + p, PAD - k : PAD - k + width, :]
                    )
                dst[z + p] = value
            return carry

        lax.fori_loop(0, 2, planes, 0)

    def vertical(ch, n, z):
        total = stencil_coef[1] * (v_buf[ch, n, z + HALO + 1] + v_buf[ch, n, z + HALO - 1])
        for k in range(2, 5):
            total = total + stencil_coef[k] * (v_buf[ch, n, z + HALO + k] + v_buf[ch, n, z + HALO - k])
        return total

    def sweep(body, ch, n):
        lax.fori_loop(0, HALO, body, 0)
        if n is not None:
            send_down(ch, n)
        lax.fori_loop(HALO, depth, body, 0)
        if n is not None:
            send_up(ch, n)

    for h in range(n_dom):
        wait_got(recv_buf.at[h], a2a_recv.at[h])
    start_swap(4)
    rows = recv_buf.shape[1]
    half = n_dom // 2
    per = max(1, rows // width)
    cut = min(rows, width)

    def unpack(p, carry):
        older = recv_buf[ints_s[0, p]].astype(F32)
        newer = recv_buf[ints_s[0, p + half]].astype(F32)
        if rows >= width:
            for j in range(per):
                u_first[p * per + j] = older[j * width : (j + 1) * width]
                put_field(0, 0, p * per + j, newer[j * width : (j + 1) * width])
        else:
            parts_of = width // cut
            z, at = p // parts_of, (p % parts_of) * cut
            at = pl.multiple_of(at, cut)
            u_first[z, pl.ds(at, cut), :] = older
            v_buf[0, 0, z + HALO, pl.ds(at, cut), :] = newer
            e_buf[0, z, pl.ds(at + PAD, cut), :] = newer
        return carry

    lax.fori_loop(0, half, unpack, 0)
    send_down(0, 0)
    send_up(0, 0)
    lateral(0, lap.at[0])

    def forward_step(n):
        last = n == STEPS - 1
        wait_halo(0, n)

        def plane(z, carry):
            value = lap[n, z] + vertical(0, n, z)
            lap[n, z] = value
            if not last:
                older = u_first[z] if n == 0 else v_buf[0, n - 1, z + HALO]
                amount = floats_w[n : n + 1, n_rec : n_rec + lanes] * jnp.where(src_plane == z, 1.0, 0.0)
                put_field(
                    0,
                    n + 1,
                    z,
                    2.0 * v_buf[0, n, z + HALO] - older + speed[z] * value + src_mask[...] * amount,
                )
            return carry

        sweep(plane, 0, None if last else n + 1)
        if not last:
            lateral(0, lap.at[n + 1])

    def adjoint_step(n):
        last = n == STEPS - 1
        wait_halo(1, n)

        def plane(z, carry):
            older = lam_next[z] if n == 0 else lam[n - 1, z]
            value = 2.0 * lam[n, z] - older + (lap_adj[z] + vertical(1, n, z)) + inject[n, z]
            if last:
                lam_out[z] = value
            else:
                lam[n + 1, z] = value
                put_field(1, n + 1, z, speed[z] * value)
            return carry

        sweep(plane, 1, None if last else n + 1)

    wait_swap(2)
    forward_step(0)
    wait_swap(3)

    def first_scaled(z, carry):
        put_field(1, 0, z, speed[z] * lam[0, z])
        return carry

    sweep(first_scaled, 1, 0)
    lateral(1, lap_adj)
    forward_step(1)
    wait_swap(4)
    start_swap(7)
    adjoint_step(0)
    lateral(1, lap_adj)
    forward_step(2)
    adjoint_step(1)
    lateral(1, lap_adj)
    forward_step(3)

    def early_terms(z, carry):
        total = lam[0, z] * lap[STEPS - 1, z]
        for k in range(1, STEPS - 1):
            total = total + lam[k, z] * lap[STEPS - 1 - k, z]
        grad_part[z] = total
        return carry

    lax.fori_loop(0, depth, early_terms, 0)
    start_swap(8)
    adjoint_step(2)
    start_swap(5)
    lateral(1, lap_adj)
    adjoint_step(3)
    start_swap(6)

    wait_swap(7)
    wait_swap(8)
    wait_swap(5)

    def gradient(z, carry):
        total = grad_scale * (grad_part_w[z] + late_out[z] * lap_w[z])
        for j in range(n_shot):
            grad_send[j, z] = total[j * share : (j + 1) * share]
        return carry

    lax.fori_loop(0, depth, gradient, 0)

    def share_to(i):
        j = (shot + i) % n_shot
        return remote(grad_send.at[j], grad_recv.at[shot], grad_ssem.at[j], grad_rsem.at[shot], (j, dom))

    for i in range(1, n_shot):
        share_to(i).start()
    total = grad_send[shot]
    for i in range(1, n_shot):
        j = (shot + i) % n_shot
        wait_got(grad_recv.at[j], grad_rsem.at[j])
        total = total + grad_recv[j]
    grad_out[...] = total
    wait_swap(6)

    for i, (src, dst) in enumerate(swaps):
        wait_sent(same, src, dst, swap_send.at[i], swap_recv.at[i], partner)

    def piece_sent(o, carry):
        here, to = piece_to(o)
        wait_sent(here, send_buf.at[o], recv_buf.at[dom], a2a_send.at[o], a2a_recv.at[dom], to)
        return carry

    lax.fori_loop(0, n_dom, piece_sent, 0)
    for i in range(1, n_shot):
        share_to(i).wait_send()

    @pl.when(has_down)
    def _():
        for ch in range(2):
            for n in range(STEPS):
                to_down(ch, n).wait_send()

    @pl.when(has_up)
    def _():
        for ch in range(2):
            for n in range(STEPS):
                to_up(ch, n).wait_send()


def per_device(
    n_shot,
    n_dom,
    parked,
    parked_slot,
    holder_list,
    speed_sq,
    adjoint_next,
    adjoint_now,
    wavelet,
    src_depth,
    src_row,
    rec_depth,
    rec_row,
    residuals,
):
    depth, width, lanes = speed_sq.shape
    n_rec = rec_depth.shape[0]
    piece = parked.shape[2]
    rows = piece // lanes
    pieces = parked[0].reshape(n_dom, rows, lanes)
    vmem = pl.BlockSpec(memory_space=pltpu.VMEM)
    smem = pl.BlockSpec(memory_space=pltpu.SMEM)
    anywhere = pl.BlockSpec(memory_space=pl.ANY)
    slab = (depth, width, lanes)
    dma = pltpu.SemaphoreType.DMA
    share = width // n_shot
    grad, late, early = pl.pallas_call(
        functools.partial(window_kernel, n_shot, n_dom),
        out_shape=[
            jax.ShapeDtypeStruct((depth, share, lanes), F32),
            jax.ShapeDtypeStruct(slab, F32),
            jax.ShapeDtypeStruct(slab, F32),
        ],
        in_specs=[vmem] + [smem] * 5 + [vmem] + [anywhere] * 3 + [vmem] * 2,
        out_specs=[vmem] * 3,
        scratch_shapes=[
            pltpu.VMEM((n_dom, rows, lanes), BF16),
            pltpu.VMEM((n_dom, rows, lanes), BF16),
            pltpu.VMEM((8, 128), jnp.int32),
            pltpu.VMEM((8, n_rec + lanes), F32),
            pltpu.VMEM((8, 128), jnp.int32),
            pltpu.SMEM((8, 128), jnp.int32),
            pltpu.VMEM((8, n_rec + lanes), F32),
            pltpu.VMEM(slab, F32),
            pltpu.VMEM(slab, F32),
            pltpu.VMEM((STEPS,) + slab, F32),
            pltpu.VMEM(slab, F32),
            pltpu.VMEM((2, STEPS, depth + 2 * HALO, width, lanes), F32),
            pltpu.VMEM((2, depth, width + 2 * PAD, lanes), F32),
            pltpu.VMEM((STEPS,) + slab, F32),
            pltpu.VMEM(slab, F32),
            pltpu.VMEM((4 * lanes, lanes), BF16),
            pltpu.VMEM((2, STEPS * lanes, n_rec), BF16),
            pltpu.VMEM((STEPS,) + slab, F32),
            pltpu.VMEM((width, lanes), F32),
            pltpu.VMEM((n_shot, depth, share, lanes), F32),
            pltpu.VMEM((n_shot, depth, share, lanes), F32),
            pltpu.VMEM(slab, F32),
            pltpu.VMEM(slab, F32),
            pltpu.VMEM(slab, F32),
            pltpu.VMEM(slab, F32),
            dma((n_dom,)),
            dma((n_dom,)),
            dma((9,)),
            dma((9,)),
            dma((4 * STEPS,)),
            dma((4 * STEPS,)),
            dma((n_shot,)),
            dma((n_shot,)),
            dma,
        ],
        compiler_params=pltpu.CompilerParams(
            collective_id=0, has_side_effects=True, vmem_limit_bytes=VMEM_BYTES
        ),
        name="adjoint_window",
    )(
        pieces,
        parked_slot[0, 0],
        holder_list[0, 0],
        wavelet[0],
        src_depth,
        src_row,
        residuals[0],
        speed_sq,
        adjoint_next[0],
        adjoint_now[0],
        rec_depth[None],
        rec_row[None],
    )
    return grad, late[None], early[None]


def solution(mesh):
    n_shot, n_dom = mesh.shape["shot"], mesh.shape["dom"]
    in_specs = (
        P("shot", "dom", None),
        P("shot", "dom", None),
        P("shot", "dom", None),
        P("dom", None, None),
        P("shot", "dom", None, None),
        P("shot", "dom", None, None),
        P("shot", None),
        P("shot"),
        P("shot"),
        P(),
        P(),
        P("shot", None, None),
    )
    out_specs = (P("dom", "shot", None), P("shot", "dom", None, None), P("shot", "dom", None, None))
    return jax.shard_map(
        functools.partial(per_device, n_shot, n_dom),
        mesh=mesh,
        in_specs=in_specs,
        out_specs=out_specs,
        check_vma=False,
    )
```

```python
import functools

import jax
import jax.numpy as jnp
from jax import lax
from jax.experimental import pallas as pl
from jax.experimental.pallas import tpu as pltpu
from jax.sharding import PartitionSpec as P

STEPS = 4
HALO = 4
PAD = 8
VMEM_BYTES = 48 * 1024 * 1024

stencil_coef = (-205.0 / 72.0, 8.0 / 5.0, -1.0 / 5.0, 8.0 / 315.0, -1.0 / 560.0)
grad_scale = 0.0625

MESH = pl.DeviceIdType.MESH
F32 = jnp.float32
BF16 = jnp.bfloat16


def split2(value):
    high = value.astype(BF16)
    return high, (value - high.astype(F32)).astype(BF16)


def window_kernel(
    n_shot,
    n_dom,
    parked,
    slot,
    holder,
    wavelet,
    src_depth,
    src_row,
    residuals,
    speed_in,
    next_in,
    now_in,
    rec_depth,
    rec_row,
    grad_out,
    late_out,
    early_out,
    send_buf,
    recv_buf,
    ints,
    floats,
    ints_w,
    ints_s,
    floats_w,
    speed,
    lam_next,
    lam,
    u_first,
    v_buf,
    e_buf,
    lap,
    lap_adj,
    band,
    parts,
    inject,
    src_mask,
    grad_send,
    grad_recv,
    lam_out,
    grad_part,
    a2a_send,
    a2a_recv,
    swap_send,
    swap_recv,
    halo_send,
    halo_recv,
    grad_ssem,
    grad_rsem,
    local_sem,
):
    depth, width, lanes = speed_in.shape
    groups = n_shot // 2
    share = width // n_shot
    n_rec = rec_depth.shape[1]
    shot = lax.axis_index("shot")
    dom = lax.axis_index("dom")
    a, c = shot // 2, shot % 2
    b, y = dom // 2, dom % 2
    same = c == y
    my_shot = 2 * a + y
    my_dom = 2 * b + c
    partner = (2 * a + y, 2 * b + c)

    lane = lax.broadcasted_iota(jnp.int32, (8, 128), 1)
    line = lax.broadcasted_iota(jnp.int32, (8, 128), 0)
    first = lax.fori_loop(
        0, n_dom, lambda p, v: jnp.where(lane == p, holder[p], v), jnp.zeros((8, 128), jnp.int32)
    )
    second = jnp.where(lane == 0, src_depth[0], src_row[0])
    ints[...] = jnp.where(line == 0, first, second)
    floats[0:STEPS, 0:n_rec] = residuals[...]
    for n in range(STEPS - 1):
        floats[n : n + 1, n_rec : n_rec + lanes] = jnp.full((1, lanes), wavelet[n], F32)
    floats[STEPS - 1 : STEPS, n_rec : n_rec + lanes] = jnp.zeros((1, lanes), F32)
    floats[STEPS:8, :] = jnp.zeros((8 - STEPS, n_rec + lanes), F32)

    barrier = pltpu.get_barrier_semaphore()

    def greet(shot_to, dom_to):
        pl.semaphore_signal(barrier, inc=1, device_id=(shot_to, dom_to), device_id_type=MESH)

    def greet_dom(i, carry):
        to = (dom + i) % n_dom
        greet(2 * a + c, to)
        greet(2 * a + 1 - c, to)
        return carry

    lax.fori_loop(1, n_dom, greet_dom, 0)
    greet(2 * a + 1 - c, dom)
    for i in range(1, groups):
        other = (a + i) % groups
        for cc in range(2):
            for yy in range(2):
                greet(2 * other + cc, 2 * b + yy)

    pl.semaphore_wait(barrier, 2 * n_dom - 1 + 4 * (groups - 1))

    def remote(src, dst, ssem, rsem, to):
        return pltpu.make_async_remote_copy(
            src_ref=src, dst_ref=dst, send_sem=ssem, recv_sem=rsem, device_id=to, device_id_type=MESH
        )

    def start_to(here, src, dst, ssem, rsem, to):
        @pl.when(here)
        def _():
            pltpu.make_async_copy(src, dst, rsem).start()

        @pl.when(jnp.logical_not(here))
        def _():
            remote(src, dst, ssem, rsem, to).start()

    def wait_sent(here, src, dst, ssem, rsem, to):
        @pl.when(jnp.logical_not(here))
        def _():
            remote(src, dst, ssem, rsem, to).wait_send()

    def wait_got(dst, rsem):
        pltpu.make_async_copy(dst, dst, rsem).wait()

    swaps = [
        (floats, floats_w),
        (ints, ints_w),
        (speed_in, speed),
        (now_in, lam.at[0]),
        (next_in, lam_next),
        (lam.at[STEPS - 1], late_out),
        (lam_out, early_out),
    ]

    def start_swap(i):
        start_to(same, swaps[i][0], swaps[i][1], swap_send.at[i], swap_recv.at[i], partner)

    def wait_swap(i):
        wait_got(swaps[i][1], swap_recv.at[i])

    start_swap(0)
    start_swap(1)

    def piece_to(o):
        here = jnp.logical_and(same, o == dom)
        return here, (2 * a + o % 2, 2 * (o // 2) + c)

    def send_piece(i, carry):
        o = (dom + i) % n_dom
        here, to = piece_to(o)
        send_buf[o] = parked[slot[o]]
        start_to(here, send_buf.at[o], recv_buf.at[dom], a2a_send.at[o], a2a_recv.at[dom], to)
        return carry

    start_swap(2)
    start_swap(3)

    @pl.when(same)
    def _():
        lax.fori_loop(1, n_dom + 1, send_piece, 0)


    row_i = lax.broadcasted_iota(jnp.int32, (lanes, lanes), 0)
    col_i = lax.broadcasted_iota(jnp.int32, (lanes, lanes), 1)
    apart = jnp.abs(row_i - col_i)
    matrix = jnp.zeros((lanes, lanes), F32)
    for k in range(1, 5):
        matrix = jnp.where(apart == k, stencil_coef[k], matrix)
    m_high, m_low = split2(matrix)
    for i, part in enumerate((m_high, m_high, m_low, m_low)):
        band[i * lanes : (i + 1) * lanes, :] = part
    zeros_pad = jnp.zeros((depth, PAD, lanes), F32)
    for ch in range(2):
        e_buf[ch, :, 0:PAD, :] = zeros_pad
        e_buf[ch, :, PAD + width : 2 * PAD + width, :] = zeros_pad

    has_down = my_dom > 0
    has_up = my_dom < n_dom - 1
    top = 4 + depth

    @pl.when(jnp.logical_not(has_down))
    def _():
        def clear(i, carry):
            v_buf[i // STEPS, i % STEPS, 0:HALO] = jnp.zeros((HALO, width, lanes), F32)
            return carry

        lax.fori_loop(0, 2 * STEPS, clear, 0)

    @pl.when(jnp.logical_not(has_up))
    def _():
        def clear(i, carry):
            v_buf[i // STEPS, i % STEPS, top : top + HALO] = jnp.zeros((HALO, width, lanes), F32)
            return carry

        lax.fori_loop(0, 2 * STEPS, clear, 0)

    local_depth = rec_depth[...] - my_dom * depth
    rec_line = local_depth * width + rec_row[...] // lanes
    rec_lane = rec_row[...] % lanes
    wait_swap(0)
    wait_swap(1)
    to_scalar = pltpu.make_async_copy(ints_w, ints_s, local_sem)
    to_scalar.start()
    lane_hit = lax.broadcasted_iota(jnp.int32, (lanes, n_rec), 0) == rec_lane
    for k in range(STEPS):
        amounts = jnp.where(lane_hit, floats_w[k : k + 1, 0:n_rec], 0.0)
        for i, part in enumerate(split2(amounts)):
            parts[i, k * lanes : (k + 1) * lanes, :] = part
    to_scalar.wait()

    start_swap(4)
    group = depth // 2

    def inject_half(h, carry):
        line = lax.broadcasted_iota(jnp.int32, (group * width, n_rec), 0) + h * (group * width)
        hit = jnp.where(line == rec_line, 1.0, 0.0).astype(BF16)
        total = jnp.zeros((group * width, STEPS * lanes), F32)
        for i in range(2):
            total = total + lax.dot_general(
                hit, parts[i], (((1,), (1,)), ((), ())), preferred_element_type=F32
            )
        for k in range(STEPS):
            for z in range(group):
                inject[k, h * group + z] = total[z * width : (z + 1) * width, k * lanes : (k + 1) * lanes]
        return carry

    lax.fori_loop(0, 2, inject_half, 0)

    src_plane = ints_s[1, 0] - my_dom * depth
    cell = lax.broadcasted_iota(jnp.int32, (width, lanes), 0) * lanes + lax.broadcasted_iota(
        jnp.int32, (width, lanes), 1
    )
    src_mask[...] = jnp.where(cell == ints_s[1, 1], 1.0, 0.0)

    down = (2 * a + (my_dom - 1) % 2, 2 * ((my_dom + 1) // 2 - 1) + y)
    up = (2 * a + (my_dom + 1) % 2, 2 * ((my_dom + 1) // 2) + y)

    def to_down(ch, n):
        i = (ch * STEPS + n) * 2
        v = v_buf.at[ch, n]
        return remote(
            v.at[pl.ds(HALO, HALO)], v.at[pl.ds(top, HALO)], halo_send.at[i], halo_recv.at[i + 1], down
        )

    def to_up(ch, n):
        i = (ch * STEPS + n) * 2
        v = v_buf.at[ch, n]
        return remote(
            v.at[pl.ds(top - HALO, HALO)], v.at[pl.ds(0, HALO)], halo_send.at[i + 1], halo_recv.at[i], up
        )

    def send_down(ch, n):
        @pl.when(has_down)
        def _():
            to_down(ch, n).start()

    def send_up(ch, n):
        @pl.when(has_up)
        def _():
            to_up(ch, n).start()

    def wait_halo(ch, n):
        i = (ch * STEPS + n) * 2
        v = v_buf.at[ch, n]

        @pl.when(has_down)
        def _():
            wait_got(v.at[pl.ds(0, HALO)], halo_recv.at[i])

        @pl.when(has_up)
        def _():
            wait_got(v.at[pl.ds(top, HALO)], halo_recv.at[i + 1])

    def put_field(ch, n, z, value):
        v_buf[ch, n, z + HALO] = value
        e_buf[ch, z, PAD : PAD + width, :] = value

    def lateral(ch, dst):
        def planes(h, carry):
            z = h * group
            own = e_buf[ch, pl.ds(z, group), PAD : PAD + width, :]
            high, low = split2(own.reshape(group * width, lanes))
            total = jnp.dot(
                jnp.concatenate([high, low, high, low], axis=1), band[...], preferred_element_type=F32
            ).reshape(group, width, lanes)
            for p in range(group):
                value = total[p] + 3.0 * stencil_coef[0] * own[p]
                for k in range(1, 5):
                    value = value + stencil_coef[k] * (
                        e_buf[ch, z + p, PAD + k : PAD + k + width, :]
                        + e_buf[ch, z + p, PAD - k : PAD - k + width, :]
                    )
                dst[z + p] = value
            return carry

        lax.fori_loop(0, 2, planes, 0)

    def vertical(ch, n, z):
        total = stencil_coef[1] * (v_buf[ch, n, z + HALO + 1] + v_buf[ch, n, z + HALO - 1])
        for k in range(2, 5):
            total = total + stencil_coef[k] * (v_buf[ch, n, z + HALO + k] + v_buf[ch, n, z + HALO - k])
        return total

    def sweep(body, ch, n):
        lax.fori_loop(0, HALO, body, 0)
        if n is not None:
            send_down(ch, n)
        lax.fori_loop(HALO, depth, body, 0)
        if n is not None:
            send_up(ch, n)

    rows = recv_buf.shape[1]
    half = n_dom // 2
    per = max(1, rows // width)
    cut = min(rows, width)

    def unpack(p, carry):
        older = recv_buf[ints_s[0, p]].astype(F32)
        newer = recv_buf[ints_s[0, p + half]].astype(F32)
        if rows >= width:
            for j in range(per):
                u_first[p * per + j] = older[j * width : (j + 1) * width]
                put_field(0, 0, p * per + j, newer[j * width : (j + 1) * width])
        else:
            parts_of = width // cut
            z, at = p // parts_of, (p % parts_of) * cut
            at = pl.multiple_of(at, cut)
            u_first[z, pl.ds(at, cut), :] = older
            v_buf[0, 0, z + HALO, pl.ds(at, cut), :] = newer
            e_buf[0, z, pl.ds(at + PAD, cut), :] = newer
        return carry

    def first_forward():
        for h in range(n_dom):
            wait_got(recv_buf.at[h], a2a_recv.at[h])
        lax.fori_loop(0, half, unpack, 0)
        send_down(0, 0)
        send_up(0, 0)
        lateral(0, lap.at[0])

    def forward_step(n):
        wait_halo(0, n)

        def plane(z, carry):
            value = lap[n, z] + vertical(0, n, z)
            lap[n, z] = value
            older = u_first[z] if n == 0 else v_buf[0, n - 1, z + HALO]
            amount = floats_w[n : n + 1, n_rec : n_rec + lanes] * jnp.where(src_plane == z, 1.0, 0.0)
            put_field(
                0,
                n + 1,
                z,
                2.0 * v_buf[0, n, z + HALO] - older + speed[z] * value + src_mask[...] * amount,
            )
            return carry

        sweep(plane, 0, n + 1)
        lateral(0, lap.at[n + 1])

    def adjoint_step(n):
        last = n == STEPS - 1
        wait_halo(1, n)

        def plane(z, carry):
            older = lam_next[z] if n == 0 else lam[n - 1, z]
            value = 2.0 * lam[n, z] - older + (lap_adj[z] + vertical(1, n, z)) + inject[n, z]
            if last:
                lam_out[z] = value
            else:
                lam[n + 1, z] = value
                put_field(1, n + 1, z, speed[z] * value)
            return carry

        sweep(plane, 1, None if last else n + 1)

    wait_swap(2)
    wait_swap(3)

    def first_scaled(z, carry):
        put_field(1, 0, z, speed[z] * lam[0, z])
        return carry

    sweep(first_scaled, 1, 0)

    @pl.when(jnp.logical_not(same))
    def _():
        lax.fori_loop(1, n_dom + 1, send_piece, 0)

    lateral(1, lap_adj)
    wait_swap(4)
    adjoint_step(0)
    lateral(1, lap_adj)
    first_forward()
    adjoint_step(1)
    lateral(1, lap_adj)
    forward_step(0)
    adjoint_step(2)
    start_swap(5)
    lateral(1, lap_adj)
    forward_step(1)
    adjoint_step(3)
    start_swap(6)
    forward_step(2)

    def early_terms(z, carry):
        total = lam[1, z] * lap[STEPS - 2, z]
        for k in range(2, STEPS):
            total = total + lam[k, z] * lap[STEPS - 1 - k, z]
        grad_part[z] = total
        return carry

    lax.fori_loop(0, depth, early_terms, 0)
    wait_halo(0, STEPS - 1)

    def gradient(z, carry):
        value = lap[STEPS - 1, z] + vertical(0, STEPS - 1, z)
        total = grad_scale * (grad_part[z] + lam[0, z] * value)
        for j in range(n_shot):
            grad_send[j, z] = total[j * share : (j + 1) * share]
        return carry

    def share_to(j, h):
        planes = pl.ds(h * group, group)
        return (
            jnp.logical_and(same, shot == j),
            grad_send.at[j, planes],
            grad_recv.at[my_shot, planes],
            grad_ssem.at[2 * j + h],
            grad_rsem.at[2 * my_shot + h],
            (j, my_dom),
        )

    for h in range(2):
        lax.fori_loop(h * group, (h + 1) * group, gradient, 0)
        for j in range(n_shot):
            start_to(*share_to(j, h))
    for h in range(2):
        for j in range(n_shot):
            wait_got(grad_recv.at[j, pl.ds(h * group, group)], grad_rsem.at[2 * j + h])
        total = grad_recv[0, h * group : (h + 1) * group]
        for j in range(1, n_shot):
            total = total + grad_recv[j, h * group : (h + 1) * group]
        grad_out[h * group : (h + 1) * group] = total
    wait_swap(5)
    wait_swap(6)

    for i, (src, dst) in enumerate(swaps):
        wait_sent(same, src, dst, swap_send.at[i], swap_recv.at[i], partner)

    def piece_sent(o, carry):
        here, to = piece_to(o)
        wait_sent(here, send_buf.at[o], recv_buf.at[dom], a2a_send.at[o], a2a_recv.at[dom], to)
        return carry

    lax.fori_loop(0, n_dom, piece_sent, 0)
    for h in range(2):
        for j in range(n_shot):
            wait_sent(*share_to(j, h))

    @pl.when(has_down)
    def _():
        for ch in range(2):
            for n in range(STEPS):
                to_down(ch, n).wait_send()

    @pl.when(has_up)
    def _():
        for ch in range(2):
            for n in range(STEPS):
                to_up(ch, n).wait_send()


def per_device(
    n_shot,
    n_dom,
    parked,
    parked_slot,
    holder_list,
    speed_sq,
    adjoint_next,
    adjoint_now,
    wavelet,
    src_depth,
    src_row,
    rec_depth,
    rec_row,
    residuals,
):
    depth, width, lanes = speed_sq.shape
    n_rec = rec_depth.shape[0]
    piece = parked.shape[2]
    rows = piece // lanes
    pieces = parked[0].reshape(n_dom, rows, lanes)
    vmem = pl.BlockSpec(memory_space=pltpu.VMEM)
    smem = pl.BlockSpec(memory_space=pltpu.SMEM)
    hbm = pl.BlockSpec(memory_space=pltpu.HBM)
    slab = (depth, width, lanes)
    dma = pltpu.SemaphoreType.DMA
    share = width // n_shot
    grad, late, early = pl.pallas_call(
        functools.partial(window_kernel, n_shot, n_dom),
        out_shape=[
            jax.ShapeDtypeStruct((depth, share, lanes), F32),
            jax.ShapeDtypeStruct(slab, F32),
            jax.ShapeDtypeStruct(slab, F32),
        ],
        in_specs=[vmem] + [smem] * 5 + [vmem] + [hbm] * 3 + [vmem] * 2,
        out_specs=[vmem] * 3,
        scratch_shapes=[
            pltpu.VMEM((n_dom, rows, lanes), BF16),
            pltpu.VMEM((n_dom, rows, lanes), BF16),
            pltpu.VMEM((8, 128), jnp.int32),
            pltpu.VMEM((8, n_rec + lanes), F32),
            pltpu.VMEM((8, 128), jnp.int32),
            pltpu.SMEM((8, 128), jnp.int32),
            pltpu.VMEM((8, n_rec + lanes), F32),
            pltpu.VMEM(slab, F32),
            pltpu.VMEM(slab, F32),
            pltpu.VMEM((STEPS,) + slab, F32),
            pltpu.VMEM(slab, F32),
            pltpu.VMEM((2, STEPS, depth + 2 * HALO, width, lanes), F32),
            pltpu.VMEM((2, depth, width + 2 * PAD, lanes), F32),
            pltpu.VMEM((STEPS,) + slab, F32),
            pltpu.VMEM(slab, F32),
            pltpu.VMEM((4 * lanes, lanes), BF16),
            pltpu.VMEM((2, STEPS * lanes, n_rec), BF16),
            pltpu.VMEM((STEPS,) + slab, F32),
            pltpu.VMEM((width, lanes), F32),
            pltpu.VMEM((n_shot, depth, share, lanes), F32),
            pltpu.VMEM((n_shot, depth, share, lanes), F32),
            pltpu.VMEM(slab, F32),
            pltpu.VMEM(slab, F32),
            dma((n_dom,)),
            dma((n_dom,)),
            dma((7,)),
            dma((7,)),
            dma((4 * STEPS,)),
            dma((4 * STEPS,)),
            dma((2 * n_shot,)),
            dma((2 * n_shot,)),
            dma,
        ],
        compiler_params=pltpu.CompilerParams(
            collective_id=0, has_side_effects=True, vmem_limit_bytes=VMEM_BYTES
        ),
        name="adjoint_window",
    )(
        pieces,
        parked_slot[0, 0],
        holder_list[0, 0],
        wavelet[0],
        src_depth,
        src_row,
        residuals[0],
        speed_sq,
        adjoint_next[0],
        adjoint_now[0],
        rec_depth[None],
        rec_row[None],
    )
    return grad, late[None], early[None]


def solution(mesh):
    n_shot, n_dom = mesh.shape["shot"], mesh.shape["dom"]
    in_specs = (
        P("shot", "dom", None),
        P("shot", "dom", None),
        P("shot", "dom", None),
        P("dom", None, None),
        P("shot", "dom", None, None),
        P("shot", "dom", None, None),
        P("shot", None),
        P("shot"),
        P("shot"),
        P(),
        P(),
        P("shot", None, None),
    )
    out_specs = (P("dom", "shot", None), P("shot", "dom", None, None), P("shot", "dom", None, None))
    return jax.shard_map(
        functools.partial(per_device, n_shot, n_dom),
        mesh=mesh,
        in_specs=in_specs,
        out_specs=out_specs,
        check_vma=False,
    )
```

```python
import functools

import jax
import jax.numpy as jnp
from jax import lax
from jax.experimental import pallas as pl
from jax.experimental.pallas import tpu as pltpu
from jax.sharding import PartitionSpec as P

STEPS = 4
HALO = 4
PAD = 8
VMEM_BYTES = 48 * 1024 * 1024

stencil_coef = (-205.0 / 72.0, 8.0 / 5.0, -1.0 / 5.0, 8.0 / 315.0, -1.0 / 560.0)
grad_scale = 0.0625

MESH = pl.DeviceIdType.MESH
F32 = jnp.float32
BF16 = jnp.bfloat16


def split2(value):
    high = value.astype(BF16)
    return high, (value - high.astype(F32)).astype(BF16)


def window_kernel(
    n_shot,
    n_dom,
    parked,
    slot,
    holder,
    wavelet,
    src_depth,
    src_row,
    residuals,
    speed_in,
    next_in,
    now_in,
    rec_depth,
    rec_row,
    grad_out,
    late_out,
    early_out,
    send_buf,
    recv_buf,
    ints,
    floats,
    ints_w,
    ints_s,
    floats_w,
    speed,
    lam_next,
    lam,
    u_first,
    v_buf,
    e_buf,
    lap,
    lap_adj,
    band,
    parts,
    inject,
    src_mask,
    grad_send,
    grad_recv,
    lam_out,
    grad_part,
    a2a_send,
    a2a_recv,
    swap_send,
    swap_recv,
    halo_send,
    halo_recv,
    grad_ssem,
    grad_rsem,
    local_sem,
    pass_send,
    pass_recv,
):
    depth, width, lanes = speed_in.shape
    groups = n_shot // 2
    share = width // n_shot
    n_rec = rec_depth.shape[1]
    shot = lax.axis_index("shot")
    dom = lax.axis_index("dom")
    a, c = shot // 2, shot % 2
    b, y = dom // 2, dom % 2
    same = c == y
    my_shot = 2 * a + y
    my_dom = 2 * b + c
    partner = (2 * a + y, 2 * b + c)

    lane = lax.broadcasted_iota(jnp.int32, (8, 128), 1)
    line = lax.broadcasted_iota(jnp.int32, (8, 128), 0)
    first = lax.fori_loop(
        0, n_dom, lambda p, v: jnp.where(lane == p, holder[p], v), jnp.zeros((8, 128), jnp.int32)
    )
    second = jnp.where(lane == 0, src_depth[0], src_row[0])
    ints[...] = jnp.where(line == 0, first, second)
    floats[0:STEPS, 0:n_rec] = residuals[...]
    for n in range(STEPS - 1):
        floats[n : n + 1, n_rec : n_rec + lanes] = jnp.full((1, lanes), wavelet[n], F32)
    floats[STEPS - 1 : STEPS, n_rec : n_rec + lanes] = jnp.zeros((1, lanes), F32)
    floats[STEPS:8, :] = jnp.zeros((8 - STEPS, n_rec + lanes), F32)

    barrier = pltpu.get_barrier_semaphore()

    def greet(shot_to, dom_to):
        pl.semaphore_signal(barrier, inc=1, device_id=(shot_to, dom_to), device_id_type=MESH)

    def greet_dom(i, carry):
        to = (dom + i) % n_dom
        greet(2 * a + c, to)
        greet(2 * a + 1 - c, to)
        return carry

    lax.fori_loop(1, n_dom, greet_dom, 0)
    greet(2 * a + 1 - c, dom)
    for i in range(1, groups):
        other = (a + i) % groups
        for cc in range(2):
            for yy in range(2):
                greet(2 * other + cc, 2 * b + yy)

    pl.semaphore_wait(barrier, 2 * n_dom - 1 + 4 * (groups - 1))

    def remote(src, dst, ssem, rsem, to):
        return pltpu.make_async_remote_copy(
            src_ref=src, dst_ref=dst, send_sem=ssem, recv_sem=rsem, device_id=to, device_id_type=MESH
        )

    def start_to(here, src, dst, ssem, rsem, to):
        @pl.when(here)
        def _():
            pltpu.make_async_copy(src, dst, rsem).start()

        @pl.when(jnp.logical_not(here))
        def _():
            remote(src, dst, ssem, rsem, to).start()

    def wait_sent(here, src, dst, ssem, rsem, to):
        @pl.when(jnp.logical_not(here))
        def _():
            remote(src, dst, ssem, rsem, to).wait_send()

    def wait_got(dst, rsem):
        pltpu.make_async_copy(dst, dst, rsem).wait()

    swaps = [
        (floats, floats_w),
        (ints, ints_w),
        (speed_in, speed),
        (now_in, lam.at[0]),
        (next_in, lam_next),
        (lam.at[STEPS - 1], late_out),
        (lam_out, early_out),
    ]

    def start_swap(i):
        start_to(same, swaps[i][0], swaps[i][1], swap_send.at[i], swap_recv.at[i], partner)

    def wait_swap(i):
        wait_got(swaps[i][1], swap_recv.at[i])

    start_swap(0)
    start_swap(1)

    def piece_to(o):
        here = jnp.logical_and(same, o == dom)
        return here, (2 * a + o % 2, 2 * (o // 2) + c)

    def send_piece(i, carry):
        o = (dom + i) % n_dom
        here, to = piece_to(o)
        send_buf[o] = parked[slot[o]]
        start_to(here, send_buf.at[o], recv_buf.at[dom], a2a_send.at[o], a2a_recv.at[dom], to)
        return carry

    part = depth // 2
    mine = pl.ds((a % 2) * part, part)
    theirs = pl.ds((1 - a % 2) * part, part)
    next_group = (2 * (a + 1 - 2 * (a % 2)) + c, dom)
    half_speed = remote(speed_in.at[mine], speed.at[mine], swap_send.at[2], swap_recv.at[2], partner)
    pass_speed = remote(speed.at[mine], speed.at[mine], pass_send.at[0], pass_recv.at[0], next_group)

    @pl.when(same)
    def _():
        pltpu.make_async_copy(speed_in, speed, swap_recv.at[2]).start()

    @pl.when(jnp.logical_not(same))
    def _():
        half_speed.start()

    start_swap(3)

    @pl.when(same)
    def _():
        lax.fori_loop(1, n_dom + 1, send_piece, 0)


    row_i = lax.broadcasted_iota(jnp.int32, (lanes, lanes), 0)
    col_i = lax.broadcasted_iota(jnp.int32, (lanes, lanes), 1)
    apart = jnp.abs(row_i - col_i)
    matrix = jnp.zeros((lanes, lanes), F32)
    for k in range(1, 5):
        matrix = jnp.where(apart == k, stencil_coef[k], matrix)
    m_high, m_low = split2(matrix)
    for i, part in enumerate((m_high, m_high, m_low, m_low)):
        band[i * lanes : (i + 1) * lanes, :] = part
    zeros_pad = jnp.zeros((depth, PAD, lanes), F32)
    for ch in range(2):
        e_buf[ch, :, 0:PAD, :] = zeros_pad
        e_buf[ch, :, PAD + width : 2 * PAD + width, :] = zeros_pad

    has_down = my_dom > 0
    has_up = my_dom < n_dom - 1
    top = 4 + depth

    @pl.when(jnp.logical_not(has_down))
    def _():
        def clear(i, carry):
            v_buf[i // STEPS, i % STEPS, 0:HALO] = jnp.zeros((HALO, width, lanes), F32)
            return carry

        lax.fori_loop(0, 2 * STEPS, clear, 0)

    @pl.when(jnp.logical_not(has_up))
    def _():
        def clear(i, carry):
            v_buf[i // STEPS, i % STEPS, top : top + HALO] = jnp.zeros((HALO, width, lanes), F32)
            return carry

        lax.fori_loop(0, 2 * STEPS, clear, 0)

    local_depth = rec_depth[...] - my_dom * depth
    rec_line = local_depth * width + rec_row[...] // lanes
    rec_lane = rec_row[...] % lanes
    wait_swap(0)
    wait_swap(1)
    to_scalar = pltpu.make_async_copy(ints_w, ints_s, local_sem)
    to_scalar.start()

    @pl.when(jnp.logical_not(same))
    def _():
        wait_got(speed.at[mine], swap_recv.at[2])
        pass_speed.start()

    lane_hit = lax.broadcasted_iota(jnp.int32, (lanes, n_rec), 0) == rec_lane
    for k in range(STEPS):
        amounts = jnp.where(lane_hit, floats_w[k : k + 1, 0:n_rec], 0.0)
        for i, part in enumerate(split2(amounts)):
            parts[i, k * lanes : (k + 1) * lanes, :] = part
    to_scalar.wait()

    start_swap(4)
    group = depth // 2

    def inject_half(h, carry):
        line = lax.broadcasted_iota(jnp.int32, (group * width, n_rec), 0) + h * (group * width)
        hit = jnp.where(line == rec_line, 1.0, 0.0).astype(BF16)
        total = jnp.zeros((group * width, STEPS * lanes), F32)
        for i in range(2):
            total = total + lax.dot_general(
                hit, parts[i], (((1,), (1,)), ((), ())), preferred_element_type=F32
            )
        for k in range(STEPS):
            for z in range(group):
                inject[k, h * group + z] = total[z * width : (z + 1) * width, k * lanes : (k + 1) * lanes]
        return carry

    lax.fori_loop(0, 2, inject_half, 0)

    src_plane = ints_s[1, 0] - my_dom * depth
    cell = lax.broadcasted_iota(jnp.int32, (width, lanes), 0) * lanes + lax.broadcasted_iota(
        jnp.int32, (width, lanes), 1
    )
    src_mask[...] = jnp.where(cell == ints_s[1, 1], 1.0, 0.0)

    down = (2 * a + (my_dom - 1) % 2, 2 * ((my_dom + 1) // 2 - 1) + y)
    up = (2 * a + (my_dom + 1) % 2, 2 * ((my_dom + 1) // 2) + y)

    def to_down(ch, n):
        i = (ch * STEPS + n) * 2
        v = v_buf.at[ch, n]
        return remote(
            v.at[pl.ds(HALO, HALO)], v.at[pl.ds(top, HALO)], halo_send.at[i], halo_recv.at[i + 1], down
        )

    def to_up(ch, n):
        i = (ch * STEPS + n) * 2
        v = v_buf.at[ch, n]
        return remote(
            v.at[pl.ds(top - HALO, HALO)], v.at[pl.ds(0, HALO)], halo_send.at[i + 1], halo_recv.at[i], up
        )

    def send_down(ch, n):
        @pl.when(has_down)
        def _():
            to_down(ch, n).start()

    def send_up(ch, n):
        @pl.when(has_up)
        def _():
            to_up(ch, n).start()

    def wait_halo(ch, n):
        i = (ch * STEPS + n) * 2
        v = v_buf.at[ch, n]

        @pl.when(has_down)
        def _():
            wait_got(v.at[pl.ds(0, HALO)], halo_recv.at[i])

        @pl.when(has_up)
        def _():
            wait_got(v.at[pl.ds(top, HALO)], halo_recv.at[i + 1])

    def put_field(ch, n, z, value):
        v_buf[ch, n, z + HALO] = value
        e_buf[ch, z, PAD : PAD + width, :] = value

    def lateral(ch, dst):
        def planes(h, carry):
            z = h * group
            own = e_buf[ch, pl.ds(z, group), PAD : PAD + width, :]
            high, low = split2(own.reshape(group * width, lanes))
            total = jnp.dot(
                jnp.concatenate([high, low, high, low], axis=1), band[...], preferred_element_type=F32
            ).reshape(group, width, lanes)
            for p in range(group):
                value = total[p] + 3.0 * stencil_coef[0] * own[p]
                for k in range(1, 5):
                    value = value + stencil_coef[k] * (
                        e_buf[ch, z + p, PAD + k : PAD + k + width, :]
                        + e_buf[ch, z + p, PAD - k : PAD - k + width, :]
                    )
                dst[z + p] = value
            return carry

        lax.fori_loop(0, 2, planes, 0)

    def vertical(ch, n, z):
        total = stencil_coef[1] * (v_buf[ch, n, z + HALO + 1] + v_buf[ch, n, z + HALO - 1])
        for k in range(2, 5):
            total = total + stencil_coef[k] * (v_buf[ch, n, z + HALO + k] + v_buf[ch, n, z + HALO - k])
        return total

    def sweep(body, ch, n):
        lax.fori_loop(0, HALO, body, 0)
        if n is not None:
            send_down(ch, n)
        lax.fori_loop(HALO, depth, body, 0)
        if n is not None:
            send_up(ch, n)

    rows = recv_buf.shape[1]
    half = n_dom // 2
    per = max(1, rows // width)
    cut = min(rows, width)

    def unpack(p, carry):
        older = recv_buf[ints_s[0, p]].astype(F32)
        newer = recv_buf[ints_s[0, p + half]].astype(F32)
        if rows >= width:
            for j in range(per):
                u_first[p * per + j] = older[j * width : (j + 1) * width]
                put_field(0, 0, p * per + j, newer[j * width : (j + 1) * width])
        else:
            parts_of = width // cut
            z, at = p // parts_of, (p % parts_of) * cut
            at = pl.multiple_of(at, cut)
            u_first[z, pl.ds(at, cut), :] = older
            v_buf[0, 0, z + HALO, pl.ds(at, cut), :] = newer
            e_buf[0, z, pl.ds(at + PAD, cut), :] = newer
        return carry

    def first_forward():
        for h in range(n_dom):
            wait_got(recv_buf.at[h], a2a_recv.at[h])
        lax.fori_loop(0, half, unpack, 0)
        send_down(0, 0)
        send_up(0, 0)
        lateral(0, lap.at[0])

    def forward_step(n):
        wait_halo(0, n)

        def plane(z, carry):
            value = lap[n, z] + vertical(0, n, z)
            lap[n, z] = value
            older = u_first[z] if n == 0 else v_buf[0, n - 1, z + HALO]
            amount = floats_w[n : n + 1, n_rec : n_rec + lanes] * jnp.where(src_plane == z, 1.0, 0.0)
            put_field(
                0,
                n + 1,
                z,
                2.0 * v_buf[0, n, z + HALO] - older + speed[z] * value + src_mask[...] * amount,
            )
            return carry

        sweep(plane, 0, n + 1)
        lateral(0, lap.at[n + 1])

    def adjoint_step(n):
        last = n == STEPS - 1
        wait_halo(1, n)

        def plane(z, carry):
            older = lam_next[z] if n == 0 else lam[n - 1, z]
            value = 2.0 * lam[n, z] - older + (lap_adj[z] + vertical(1, n, z)) + inject[n, z]
            if last:
                lam_out[z] = value
            else:
                lam[n + 1, z] = value
                put_field(1, n + 1, z, speed[z] * value)
            return carry

        sweep(plane, 1, None if last else n + 1)

    @pl.when(same)
    def _():
        wait_got(speed, swap_recv.at[2])

    @pl.when(jnp.logical_not(same))
    def _():
        wait_got(speed.at[theirs], pass_recv.at[0])

    wait_swap(3)

    def first_scaled(z, carry):
        put_field(1, 0, z, speed[z] * lam[0, z])
        return carry

    sweep(first_scaled, 1, 0)

    @pl.when(jnp.logical_not(same))
    def _():
        lax.fori_loop(1, n_dom + 1, send_piece, 0)

    lateral(1, lap_adj)
    wait_swap(4)
    adjoint_step(0)
    lateral(1, lap_adj)
    first_forward()
    adjoint_step(1)
    lateral(1, lap_adj)
    forward_step(0)
    adjoint_step(2)
    start_swap(5)
    lateral(1, lap_adj)
    forward_step(1)
    adjoint_step(3)
    start_swap(6)
    forward_step(2)

    def early_terms(z, carry):
        total = lam[1, z] * lap[STEPS - 2, z]
        for k in range(2, STEPS):
            total = total + lam[k, z] * lap[STEPS - 1 - k, z]
        grad_part[z] = total
        return carry

    lax.fori_loop(0, depth, early_terms, 0)
    wait_halo(0, STEPS - 1)

    def gradient(z, carry):
        value = lap[STEPS - 1, z] + vertical(0, STEPS - 1, z)
        total = grad_scale * (grad_part[z] + lam[0, z] * value)
        for j in range(n_shot):
            grad_send[j, z] = total[j * share : (j + 1) * share]
        return carry

    def share_to(j, h):
        planes = pl.ds(h * group, group)
        return (
            jnp.logical_and(same, shot == j),
            grad_send.at[j, planes],
            grad_recv.at[my_shot, planes],
            grad_ssem.at[2 * j + h],
            grad_rsem.at[2 * my_shot + h],
            (j, my_dom),
        )

    for h in range(2):
        lax.fori_loop(h * group, (h + 1) * group, gradient, 0)
        for j in range(n_shot):
            start_to(*share_to(j, h))
    for h in range(2):
        for j in range(n_shot):
            wait_got(grad_recv.at[j, pl.ds(h * group, group)], grad_rsem.at[2 * j + h])
        total = grad_recv[0, h * group : (h + 1) * group]
        for j in range(1, n_shot):
            total = total + grad_recv[j, h * group : (h + 1) * group]
        grad_out[h * group : (h + 1) * group] = total
    wait_swap(5)
    wait_swap(6)

    @pl.when(jnp.logical_not(same))
    def _():
        half_speed.wait_send()
        pass_speed.wait_send()

    for i, (src, dst) in enumerate(swaps):
        if i == 2:
            continue
        wait_sent(same, src, dst, swap_send.at[i], swap_recv.at[i], partner)

    def piece_sent(o, carry):
        here, to = piece_to(o)
        wait_sent(here, send_buf.at[o], recv_buf.at[dom], a2a_send.at[o], a2a_recv.at[dom], to)
        return carry

    lax.fori_loop(0, n_dom, piece_sent, 0)
    for h in range(2):
        for j in range(n_shot):
            wait_sent(*share_to(j, h))

    @pl.when(has_down)
    def _():
        for ch in range(2):
            for n in range(STEPS):
                to_down(ch, n).wait_send()

    @pl.when(has_up)
    def _():
        for ch in range(2):
            for n in range(STEPS):
                to_up(ch, n).wait_send()


def per_device(
    n_shot,
    n_dom,
    parked,
    parked_slot,
    holder_list,
    speed_sq,
    adjoint_next,
    adjoint_now,
    wavelet,
    src_depth,
    src_row,
    rec_depth,
    rec_row,
    residuals,
):
    depth, width, lanes = speed_sq.shape
    n_rec = rec_depth.shape[0]
    piece = parked.shape[2]
    rows = piece // lanes
    pieces = parked[0].reshape(n_dom, rows, lanes)
    vmem = pl.BlockSpec(memory_space=pltpu.VMEM)
    smem = pl.BlockSpec(memory_space=pltpu.SMEM)
    hbm = pl.BlockSpec(memory_space=pltpu.HBM)
    slab = (depth, width, lanes)
    dma = pltpu.SemaphoreType.DMA
    share = width // n_shot
    grad, late, early = pl.pallas_call(
        functools.partial(window_kernel, n_shot, n_dom),
        out_shape=[
            jax.ShapeDtypeStruct((depth, share, lanes), F32),
            jax.ShapeDtypeStruct(slab, F32),
            jax.ShapeDtypeStruct(slab, F32),
        ],
        in_specs=[vmem] + [smem] * 5 + [vmem] + [hbm] * 3 + [vmem] * 2,
        out_specs=[vmem] * 3,
        scratch_shapes=[
            pltpu.VMEM((n_dom, rows, lanes), BF16),
            pltpu.VMEM((n_dom, rows, lanes), BF16),
            pltpu.VMEM((8, 128), jnp.int32),
            pltpu.VMEM((8, n_rec + lanes), F32),
            pltpu.VMEM((8, 128), jnp.int32),
            pltpu.SMEM((8, 128), jnp.int32),
            pltpu.VMEM((8, n_rec + lanes), F32),
            pltpu.VMEM(slab, F32),
            pltpu.VMEM(slab, F32),
            pltpu.VMEM((STEPS,) + slab, F32),
            pltpu.VMEM(slab, F32),
            pltpu.VMEM((2, STEPS, depth + 2 * HALO, width, lanes), F32),
            pltpu.VMEM((2, depth, width + 2 * PAD, lanes), F32),
            pltpu.VMEM((STEPS,) + slab, F32),
            pltpu.VMEM(slab, F32),
            pltpu.VMEM((4 * lanes, lanes), BF16),
            pltpu.VMEM((2, STEPS * lanes, n_rec), BF16),
            pltpu.VMEM((STEPS,) + slab, F32),
            pltpu.VMEM((width, lanes), F32),
            pltpu.VMEM((n_shot, depth, share, lanes), F32),
            pltpu.VMEM((n_shot, depth, share, lanes), F32),
            pltpu.VMEM(slab, F32),
            pltpu.VMEM(slab, F32),
            dma((n_dom,)),
            dma((n_dom,)),
            dma((7,)),
            dma((7,)),
            dma((4 * STEPS,)),
            dma((4 * STEPS,)),
            dma((2 * n_shot,)),
            dma((2 * n_shot,)),
            dma,
            dma((1,)),
            dma((1,)),
        ],
        compiler_params=pltpu.CompilerParams(
            collective_id=0, has_side_effects=True, vmem_limit_bytes=VMEM_BYTES
        ),
        name="adjoint_window",
    )(
        pieces,
        parked_slot[0, 0],
        holder_list[0, 0],
        wavelet[0],
        src_depth,
        src_row,
        residuals[0],
        speed_sq,
        adjoint_next[0],
        adjoint_now[0],
        rec_depth[None],
        rec_row[None],
    )
    return grad, late[None], early[None]


def solution(mesh):
    n_shot, n_dom = mesh.shape["shot"], mesh.shape["dom"]
    in_specs = (
        P("shot", "dom", None),
        P("shot", "dom", None),
        P("shot", "dom", None),
        P("dom", None, None),
        P("shot", "dom", None, None),
        P("shot", "dom", None, None),
        P("shot", None),
        P("shot"),
        P("shot"),
        P(),
        P(),
        P("shot", None, None),
    )
    out_specs = (P("dom", "shot", None), P("shot", "dom", None, None), P("shot", "dom", None, None))
    return jax.shard_map(
        functools.partial(per_device, n_shot, n_dom),
        mesh=mesh,
        in_specs=in_specs,
        out_specs=out_specs,
        check_vma=False,
    )
```
